512 devices in a mesh: loop: 16 (over y, x_hi), dp: 32 (over z, x_lo, core).
Axes of the slice: x: 4 (x_hi: 2, x_lo: 2; x = x_hi * 2 + x_lo), y: 8, z: 8, core: 2. Of those that a mesh axis runs over, the one named last changes fastest.
Arguments:
- images: bfloat16 [32, 32, 16, 16, 768], P('dp', 'loop'), may hold values from -6 to 6
- kernel: float32 [7, 7, 768], replicated, may hold values from -0.875 to 0.875
- ln_gain: float32 [768], replicated, may hold values from 0.5 to 1.5
- w_up: bfloat16 [768, 1536], P('dp'), may hold values from -0.21875 to 0.21875
- b_up: float32 [1536], replicated, may hold values from -3 to 3
- w_down: bfloat16 [1536, 768], P('dp'), may hold values from -0.15625 to 0.15625
- layer_scale: float32 [768], replicated, may hold values from 0.3 to 1
- w_head: bfloat16 [768, 1152], P('dp'), may hold values from -0.21875 to 0.21875
- text_rows: bfloat16 [32, 32, 1152], P('dp', 'loop'), may hold values from -6 to 6
- pair_ids: int32 [32, 32], P('dp', 'loop'), may hold values from 0 to 31, each once within a row
- log_temp: float32 [1], replicated, may hold values from 1.5 to 2.5
- loss_bias: float32 [1], replicated, may hold values from -6 to -2
Outputs:
- kernel_grad: float32 [7, 7, 768], replicated
- up_grad: float32 [768, 1536], P('dp')
- text_grad: float32 [32, 32, 1152], P('dp', 'loop')
The draws below stay inside these ranges and needn't reach their ends.
Inputs may be any that keep to these rules, and one draw needn't show every extreme that they name: Each row of pair_ids holds every index of its group once.
All inputs are finite; a program needn't handle non-finite values.
Results may differ from the reference program's by a relative error of at most 0.04.
Values may be sent and summed in bfloat16 or wider, within the bound.
A program may use at most 64 MiB of HBM per device.

```python
import jax
import jax.numpy as jnp
from jax import lax

C = 768
FFW = 1536
E = 1152
SIDE = 16
IMG_DEV = 2
GROUP = 32
N_LOOP = 16
N_DP = 32


def block_levels(stream_key, extent, cuts, least, high):
    loudness = 1.0
    for axis_at, parts in cuts:
        steps = jax.random.uniform(jax.random.fold_in(jax.random.fold_in(stream_key, 6), axis_at), (parts,), jnp.float32, least / len(cuts), high / len(cuts))
        loudness = loudness * jnp.repeat(jnp.exp(steps), extent[axis_at] // parts).reshape((-1,) + (1,) * (len(extent) - 1 - axis_at))
    return loudness


def gaussian(key, shape, deviation, bound, shards=(), kind=jnp.bfloat16):
    result = jax.random.normal(key, shape, jnp.float32) * deviation
    if len(shards) > 0:
        result = block_levels(key, shape, shards, -0.22, 0.18) * result
    return jnp.clip(result, min=-bound, max=bound).astype(kind)


def setup_inputs(seed: int = 0) -> dict:
    splits = jax.random.split(jax.random.key(seed), 13)
    images = gaussian(splits[0], (N_DP, GROUP, SIDE, SIDE, C), 1.0, 6.0, ((0, 32), (1, 16)))
    kernel = gaussian(splits[1], (7, 7, C), 49 ** -0.5, 0.875, (), jnp.float32)
    ln_gain = jnp.clip(jax.random.uniform(splits[2], (C,), jnp.float32, 0.5, 1.5), 0.5, 1.5)
    w_up = gaussian(splits[3], (C, FFW), C ** -0.5, 0.21875, ((0, 32),))
    b_up = gaussian(splits[4], (FFW,), 0.5, 3.0, (), jnp.float32)
    w_down = gaussian(splits[5], (FFW, C), FFW ** -0.5, 0.15625, ((0, 32),))
    layer_scale = jnp.clip(jax.random.uniform(splits[6], (C,), jnp.float32, 0.3, 1.0), 0.3, 1.0)
    w_head = gaussian(splits[7], (C, E), C ** -0.5, 0.21875, ((0, 32),))
    text_rows = gaussian(splits[8], (N_DP, GROUP, E), 1.0, 6.0, ((0, 32), (1, 16)))
    pair_ids = jax.vmap(lambda own: jax.random.permutation(own, GROUP))(jax.random.split(splits[9], N_DP)).reshape((N_DP, GROUP)).astype(jnp.int32)
    log_temp = jnp.clip(jax.random.uniform(splits[10], (1,), jnp.float32, 1.5, 2.5), 1.5, 2.5)
    loss_bias = jnp.clip(jax.random.uniform(splits[11], (1,), jnp.float32, -6.0, -2.0), -6.0, -2.0)
    return {"images": images, "kernel": kernel, "ln_gain": ln_gain, "w_up": w_up, "b_up": b_up, "w_down": w_down, "layer_scale": layer_scale, "w_head": w_head, "text_rows": text_rows, "pair_ids": pair_ids, "log_temp": log_temp, "loss_bias": loss_bias}


epsilon = 1e-06

def image_tower(kernel, w_up, images, ln_gain, b_up, w_down, layer_scale, w_head):
    image_count = images.shape[0]
    grid_side = images.shape[1]
    channels = images.shape[3]
    padded = jnp.pad(images, ((0, 0), (3, 3), (3, 3), (0, 0)))
    conv_out = jnp.zeros(images.shape, jnp.float32)
    for row_off in range(7):
        for col_off in range(7):
            window = padded[:, row_off:row_off + grid_side, col_off:col_off + grid_side, :]
            conv_out = conv_out + window.astype(jnp.float32) * kernel[row_off, col_off]
    chan_mean = lax.optimization_barrier(jnp.mean(conv_out, axis=-1, keepdims=True))
    centered = conv_out - chan_mean
    chan_var = lax.optimization_barrier(jnp.mean(centered * centered, axis=-1, keepdims=True))
    normed = (centered * lax.rsqrt(chan_var + epsilon) * ln_gain).astype(jnp.bfloat16)
    flat_rows = normed.reshape(-1, channels)
    hidden = jnp.dot(flat_rows, w_up, preferred_element_type=jnp.float32) + b_up
    active = jax.nn.gelu(hidden, approximate=True).astype(jnp.bfloat16)
    mlp_out = jnp.dot(active, w_down, preferred_element_type=jnp.float32)
    block_out = images.reshape(-1, channels).astype(jnp.float32) + layer_scale * mlp_out
    pooled = lax.optimization_barrier(jnp.mean(block_out.reshape(image_count, grid_side * grid_side, channels), axis=1)).astype(jnp.bfloat16)
    embedding = jnp.dot(pooled, w_head, preferred_element_type=jnp.float32)
    return embedding * lax.rsqrt(lax.optimization_barrier(jnp.sum(embedding * embedding, axis=-1, keepdims=True)) + epsilon)

def normalize(text_block):
    raw_rows = text_block.astype(jnp.float32)
    text_norm = jnp.sqrt(lax.optimization_barrier(jnp.sum(raw_rows * raw_rows, axis=-1, keepdims=True)) + epsilon)
    text_hat = raw_rows / text_norm
    rounded = lax.optimization_barrier(text_hat.astype(jnp.bfloat16))
    return (text_hat, text_norm, rounded)

def pair_grad(image_emb, text_emb, pair_row, text_index, logit_scale, logit_bias, group_size):
    logits = logit_scale * jnp.dot(image_emb, text_emb.T, precision=lax.Precision.HIGHEST) + logit_bias
    sign_of = jnp.where(pair_row[:, None] == text_index[None, :], 1.0, -1.0)
    return -sign_of * jax.nn.sigmoid(-sign_of * logits) / group_size

def reference(images, kernel, ln_gain, w_up, b_up, w_down, layer_scale, w_head, text_rows, pair_ids, log_temp, loss_bias):
    logit_scale = jnp.exp(log_temp[0])
    logit_bias = loss_bias[0]

    def run_tower(kernel_arg, up_arg, block):
        return image_tower(kernel_arg, up_arg, block, ln_gain, b_up, w_down, layer_scale, w_head)

    def group_step(totals, inputs):
        pictures, text_block, pair_row = inputs
        blocks = pictures.reshape(N_LOOP, IMG_DEV, SIDE, SIDE, C)
        image_emb = lax.map(lambda block: run_tower(kernel, w_up, block), blocks).reshape(GROUP, E)
        text_hat, text_norm, rounded = normalize(text_block)
        text_emb = rounded.astype(jnp.float32)
        text_index = jnp.arange(GROUP, dtype=jnp.int32)
        pair_weight = pair_grad(image_emb, text_emb, pair_row, text_index, logit_scale, logit_bias, GROUP)
        image_cot = logit_scale * jnp.dot(pair_weight, text_emb, precision=lax.Precision.HIGHEST)
        text_cot = logit_scale * jnp.dot(pair_weight.T, image_emb, precision=lax.Precision.HIGHEST)
        text_grad = (text_cot - text_hat * lax.optimization_barrier(jnp.sum(text_hat * text_cot, axis=-1, keepdims=True))) / text_norm

        def backward(sums, block_item):
            block, cotangent = block_item
            _, pullback = jax.vjp(lambda kernel_arg, up_arg: run_tower(kernel_arg, up_arg, block), kernel, w_up)
            kernel_part, up_part = pullback(cotangent)
            return ((sums[0] + kernel_part, sums[1] + up_part.astype(jnp.float32)), None)
        totals, _ = lax.scan(backward, totals, (blocks, image_cot.reshape(N_LOOP, IMG_DEV, E)))
        return (totals, text_grad)
    start = (jnp.zeros((7, 7, C), jnp.float32), jnp.zeros(w_up.shape, jnp.float32))
    totals, text_grad = lax.scan(group_step, start, (images, text_rows, pair_ids))
    return (totals[0], totals[1], text_grad)
```

```python
import functools

import jax
import jax.numpy as jnp
from jax import lax
from jax.experimental import pallas as pl
from jax.experimental.pallas import tpu as pltpu
from jax.sharding import PartitionSpec as P

MESH = pl.DeviceIdType.MESH
EPS = 1e-06
BF = jnp.bfloat16
F32 = jnp.float32
HI = lax.Precision.HIGHEST

N_LOOP = 16
N_DP = 32
N_Z = 8
C = 768
FFW = 1536
E = 1152
EH = 640
GROUP = 32
N_PIECE = 12
N_SLAB = 21


def nt(a, b, precision=None):
    return lax.dot_general(
        a, b, (((1,), (1,)), ((), ())), preferred_element_type=F32, precision=precision
    )


def tn(a, b):
    return lax.dot_general(a, b, (((0,), (0,)), ((), ())), preferred_element_type=F32)


def kernel_body(
    images,
    kern,
    gain,
    w_up,
    b_up,
    w_down,
    scale,
    w_head,
    text,
    pair,
    log_temp,
    loss_bias,
    kernel_out,
    up_out,
    text_out,
    up_pre,
    head_pre,
    up_buf,
    down_buf,
    head_buf,
    text_buf,
    text_all,
    taps,
    shifted,
    conv_pad,
    img_sum,
    normed,
    xhat,
    rstd,
    hid,
    gprime,
    dact,
    dhid,
    g_buf,
    rs1,
    s1,
    rs2,
    s2,
    rs3,
    p3,
    rs4,
    r4,
    fin,
    msg_buf,
    msg_all,
    kg,
    kr1,
    k1,
    kr2,
    kfin,
    w_send,
    w_recv,
    pre_send,
    pre_recv,
    text_send,
    text_recv,
    msg_send,
    msg_recv,
    r1_send,
    r1_recv,
    r2_send,
    r2_recv,
    r3_send,
    r3_recv,
    r4_send,
    r4_recv,
    r5_send,
    r5_recv,
    p1_send,
    p1_recv,
    p2_send,
    p2_recv,
    p3_send,
    p3_recv,
):
    me_loop = lax.axis_index("loop")
    me_dp = lax.axis_index("dp")
    core = lax.rem(me_dp, 2)
    xlo = lax.rem(me_dp // 2, 2)
    zed = me_dp // 4
    chip = me_dp // 2
    xhi = lax.rem(me_loop, 2)
    sib_dp = me_dp + 1 - 2 * core
    xnb_dp = me_dp + 2 - 4 * xlo
    loop_b = me_loop + 1 - 2 * xhi
    sgn = 1 - 2 * core

    def z_dp(offset):
        return lax.rem(zed + offset + N_Z, N_Z) * 4 + xlo * 2 + core

    def remote(src, dst, send, recv, loop, dp):
        return pltpu.make_async_remote_copy(
            src_ref=src,
            dst_ref=dst,
            send_sem=send,
            recv_sem=recv,
            device_id=(loop, dp),
            device_id_type=MESH,
        )

    barrier = pltpu.get_barrier_semaphore()

    @pl.loop(1, N_DP)
    def _(o):
        pl.semaphore_signal(
            barrier, inc=1, device_id=(me_loop, lax.rem(me_dp + o, N_DP)), device_id_type=MESH
        )

    @pl.loop(1, N_LOOP)
    def _(o):
        other = lax.rem(me_loop + o, N_LOOP)
        pl.semaphore_signal(barrier, inc=1, device_id=(other, me_dp), device_id_type=MESH)
        pl.semaphore_signal(barrier, inc=1, device_id=(other, sib_dp), device_id_type=MESH)

    pl.semaphore_signal(barrier, inc=1, device_id=(loop_b, xnb_dp), device_id_type=MESH)

    zero8 = jnp.zeros((8, C), F32)
    for half in range(2):
        rows = w_up[:, half * C : (half + 1) * C].astype(F32)
        up_pre[0, half] = jnp.concatenate([rows, zero8], axis=0).astype(BF)
    zero8 = jnp.zeros((8, EH), F32)
    rows = w_head[:, :EH].astype(F32)
    head_pre[0, 0] = jnp.concatenate([rows, zero8], axis=0).astype(BF)
    rows = w_head[:, EH:].astype(F32)
    rows = jnp.concatenate([rows, jnp.zeros((24, 2 * EH - E), F32)], axis=1)
    head_pre[0, 1] = jnp.concatenate([rows, zero8], axis=0).astype(BF)
    down_buf[chip, core] = w_down[...]
    text_buf[me_loop] = text[...].astype(F32)

    pl.semaphore_wait(barrier, N_DP - 1 + 2 * (N_LOOP - 1) + 1)

    slab_of = (
        lambda c, where: up_buf.at[c, where],
        lambda c, where: down_buf.at[where, c],
        lambda c, where: head_buf.at[c, where],
    )
    pending = []

    def send(copy):
        copy.start()
        pending.append(copy)

    def to_sibling(w, owner_core, where, sem):
        slab = slab_of[w](owner_core, where)
        send(remote(slab, slab, w_send.at[w, sem], w_recv.at[w, sem], me_loop, sib_dp))

    def to_x(w, where_z, sem):
        slab = slab_of[w](core, where_z * 2 + xlo)
        side = lax.rem(where_z, 2)
        target = me_loop + side * (loop_b - me_loop)
        send(remote(slab, slab, w_send.at[w, sem], w_recv.at[w, sem], target, xnb_dp))

    def to_z(w, where_z, direction, sem):
        slab = slab_of[w](core, where_z * 2 + xlo)
        send(
            remote(
                slab, slab, w_send.at[w, sem], w_recv.at[w, sem], me_loop, z_dp(direction * sgn)
            )
        )

    def await_slab(w, owner_core, where, sem):
        slab = slab_of[w](owner_core, where)
        remote(slab, slab, w_send.at[w, sem], w_recv.at[w, sem], me_loop, sib_dp).wait_recv()

    def kind_z(kind):
        offset = -kind if kind <= 4 else kind - 4
        return lax.rem(zed + offset * sgn + N_Z, N_Z)

    def begin(w):
        to_z(w, zed, 1, 0)
        to_z(w, zed, -1, 4)
        to_x(w, zed, 7)
        to_sibling(w, core, chip, 15)

    def z_arrival(w, kind):
        sem = kind - 1
        where_z = kind_z(kind)
        await_slab(w, core, where_z * 2 + xlo, sem)
        if kind in (1, 2, 3):
            to_z(w, where_z, 1, sem + 1)
        if kind in (5, 6):
            to_z(w, where_z, -1, sem + 1)
        to_x(w, where_z, 7 + kind)
        to_sibling(w, core, where_z * 2 + xlo, 15 + kind)

    def x_arrival(w, kind):
        where = kind_z(kind) * 2 + 1 - xlo
        await_slab(w, core, where, 7 + kind)
        to_sibling(w, core, where, 23 + kind)

    def turn(w, step):
        if step <= 4:
            z_arrival(w, step)
        if step <= 3:
            z_arrival(w, 4 + step)
        if step == 1:
            x_arrival(w, 0)
        if 2 <= step <= 5:
            x_arrival(w, step - 1)
        if 2 <= step <= 4:
            x_arrival(w, 3 + step)

    def finish(w):
        for kind in range(8):
            await_slab(w, 1 - core, kind_z_other(kind) * 2 + xlo, 15 + kind)
            await_slab(w, 1 - core, kind_z_other(kind) * 2 + 1 - xlo, 23 + kind)

    def kind_z_other(kind):
        offset = -kind if kind <= 4 else kind - 4
        return lax.rem(zed - offset * sgn + N_Z, N_Z)

    pre = []
    for index, ref in ((0, up_pre), (1, head_pre)):
        copy = remote(
            ref.at[0, 1 - core],
            ref.at[1, 0],
            pre_send.at[index],
            pre_recv.at[index],
            me_loop,
            sib_dp,
        )
        copy.start()
        pre.append(copy)
        if index == 0:
            begin(1)

    def text_copy(o):
        return remote(
            text_buf.at[me_loop],
            text_buf.at[me_loop],
            text_send.at[o],
            text_recv.at[o],
            lax.rem(me_loop + o, N_LOOP),
            me_dp,
        )

    def merge(index, ref, width):
        pre[index].wait_recv()
        mine = ref[0, core].astype(F32)[:24]
        theirs = ref[1, 0].astype(F32)[:24]
        first = core == 0
        joined = jnp.concatenate(
            [jnp.where(first, mine, theirs), jnp.where(first, theirs, mine)], axis=0
        )
        return joined.astype(BF)

    up_buf[core, chip] = merge(0, up_pre, C)
    begin(0)
    head_buf[core, chip] = merge(1, head_pre, EH)
    begin(2)

    @pl.loop(1, N_LOOP)
    def _(o):
        text_copy(o).start()

    width_at = lax.broadcasted_iota(jnp.int32, (16, 128), 0)

    def chunk_lanes(cb):
        return pl.ds(pl.multiple_of(cb * 128, 128), 128)

    def conv_chunk(chunk, carry):
        image, cb = chunk // 6, lax.rem(chunk, 6)
        lanes = chunk_lanes(cb)
        for a in range(7):
            for b in range(7):
                taps[a * 7 + b] = jnp.broadcast_to(kern[a, pl.ds(b, 1), lanes], (8, 128))

        def row(r, state):
            accs, total = state
            x = images[image, r, :, lanes].astype(F32)
            views = []
            for b in range(7):
                if b == 3:
                    view = x
                else:
                    view = pltpu.roll(x, (3 - b) % 16, 0)
                    inside = width_at >= 3 - b if b < 3 else width_at < 19 - b
                    view = jnp.where(inside, view, 0.0)
                shifted[chunk, b, r] = view
                views.append(view.reshape(2, 8, 128))
            fresh = []
            for j in range(7):
                acc = accs[j]
                for b in range(7):
                    acc = acc + views[b] * taps[(6 - j) * 7 + b]
                fresh.append(acc)
            conv_pad[image, r, :, lanes] = fresh[0].reshape(16, 128)
            return (tuple(fresh[1:]) + (jnp.zeros((2, 8, 128), F32),), total + views[3])

        zero = jnp.zeros((2, 8, 128), F32)
        accs, total = lax.fori_loop(0, 16, row, ((zero,) * 7, zero))
        for j in range(3):
            conv_pad[image, 16 + j, :, lanes] = accs[j].reshape(16, 128)
        img_sum[image, :, lanes] = total[0] + total[1]
        return carry

    plan = (
        ((0, 1), (1, 1)),
        ((2, 1), (0, 2)),
        ((1, 2), (2, 2), (0, 3)),
        ((1, 3), (0, 4)),
        ((2, 3), (0, 5)),
        ((1, 4), (2, 4)),
    )
    for group in range(6):
        lax.fori_loop(2 * group, 2 * group + 2, conv_chunk, 0)
        for w, step in plan[group]:
            turn(w, step)

    gain_row = gain[...]

    def norm_rows(index, carry):
        image, r = index // 16, lax.rem(index, 16)
        rows = pl.ds(pl.multiple_of(index * 16, 16), 16)
        value = conv_pad[image, r + 3]
        centered = value - jnp.mean(value, axis=-1, keepdims=True)
        inv = lax.rsqrt(jnp.mean(centered * centered, axis=-1, keepdims=True) + EPS)
        hat = centered * inv
        xhat[rows, :] = hat
        rstd[rows, :] = jnp.broadcast_to(inv, (16, 128))
        normed[rows, :] = (hat * gain_row).astype(BF)
        return carry

    lax.fori_loop(0, 32, norm_rows, 0)
    finish(0)

    c0 = 0.7978845608028654
    row_at = lax.broadcasted_iota(jnp.int32, (16, C), 0)
    means = []
    for half in range(2):
        hid[...] = jnp.dot(
            normed[...], up_buf[half].reshape(C, C), preferred_element_type=F32
        )
        if half == 0:
            turn(1, 5)
        else:
            turn(2, 5)
        bias = b_up[:, half * C : (half + 1) * C]
        image_sums = []
        for image in range(2):

            def gelu_rows(index, total):
                rows = pl.ds(pl.multiple_of(image * 256 + index * 16, 16), 16)
                h = hid[rows, :] + bias
                square = h * h
                t = jnp.tanh(c0 * h * (1.0 + 0.044715 * square))
                plus = 0.5 + 0.5 * t
                active = (h * plus).astype(BF).astype(F32)
                gprime[half, rows, :] = plus + (0.5 * c0) * h * (1.0 - t * t) * (
                    1.0 + (3 * 0.044715) * square
                )
                return total + active[:8] + active[8:]

            total = lax.fori_loop(0, 16, gelu_rows, jnp.zeros((8, C), F32))
            image_sums.append(jnp.sum(total, axis=0, keepdims=True) * (1.0 / 256))
        means.append(
            jnp.where(row_at == 0, image_sums[0], jnp.where(row_at == 1, image_sums[1], 0.0))
        )

    finish(1)
    mlp = jnp.zeros((16, C), F32)
    for half in range(2):
        high = means[half].astype(BF)
        low = (means[half] - high.astype(F32)).astype(BF)
        rows = down_buf[8 * half : 8 * half + 8].reshape(C, C)
        mlp = mlp + jnp.dot(high, rows, preferred_element_type=F32)
        mlp = mlp + jnp.dot(low, rows, preferred_element_type=F32)
    img_mean = [jnp.sum(img_sum[image], axis=0, keepdims=True) * (1.0 / 256) for image in range(2)]
    img_mean = jnp.where(row_at == 0, img_mean[0], jnp.where(row_at == 1, img_mean[1], 0.0))
    pooled = (img_mean + scale[...] * mlp).astype(BF)
    finish(2)
    raw = [
        jnp.dot(pooled, head_buf[half].reshape(C, EH), preferred_element_type=F32)
        for half in range(2)
    ]
    norm = lax.rsqrt(
        jnp.sum(raw[0] * raw[0], axis=-1, keepdims=True)
        + jnp.sum(raw[1] * raw[1], axis=-1, keepdims=True)
        + EPS
    )
    emb = jnp.concatenate([raw[0] * norm, raw[1][:, : E - EH] * norm], axis=1)

    @pl.loop(1, N_LOOP)
    def _(o):
        text_copy(o).wait_recv()

    for l in range(N_LOOP):
        text_all[2 * l : 2 * l + 2, :] = text_buf[l]
    raw_rows = text_all[...]
    text_norm = jnp.sqrt(jnp.sum(raw_rows * raw_rows, axis=-1, keepdims=True) + EPS)
    text_emb = (raw_rows / text_norm).astype(BF).astype(F32)
    logit_scale = jnp.exp(jnp.full((1, 1), log_temp[0], F32))
    logits = logit_scale * nt(emb, text_emb, HI) + loss_bias[0]
    pair_row_at = lax.broadcasted_iota(jnp.int32, (16, GROUP), 0)
    pair_col_at = lax.broadcasted_iota(jnp.int32, (16, GROUP), 1)
    own = jnp.where(pair_row_at == 0, pair[0, 0], pair[0, 1])
    signs = jnp.where(own == pair_col_at, 1.0, -1.0)
    weight = -signs * jax.nn.sigmoid(-signs * logits) / GROUP
    weight = jnp.where(pair_row_at < 2, weight, 0.0)
    image_cot = logit_scale * jnp.dot(weight, text_emb, precision=HI, preferred_element_type=F32)

    msg_buf[me_loop, :, :E] = emb[:2]
    msg_buf[me_loop, :, E:] = jnp.concatenate(
        [weight[:2], jnp.zeros((2, 128 - GROUP), F32)], axis=1
    )

    def msg_copy(o):
        return remote(
            msg_buf.at[me_loop],
            msg_buf.at[me_loop],
            msg_send.at[o],
            msg_recv.at[o],
            lax.rem(me_loop + o, N_LOOP),
            me_dp,
        )

    @pl.loop(1, N_LOOP)
    def _(o):
        msg_copy(o).start()

    d_raw = norm * (image_cot - emb * jnp.sum(image_cot * emb, axis=-1, keepdims=True))
    d_raw = d_raw.astype(BF)
    d_pooled = nt(d_raw[:, :EH], head_buf[0].reshape(C, EH)) + nt(
        d_raw[:, EH:], head_buf[1, :, :, : E - EH].reshape(C, E - EH)
    )
    d_pooled = d_pooled.astype(BF).astype(F32)
    d_mlp = (scale[...] * (d_pooled * (1.0 / 256))).astype(BF)
    for half in range(2):
        value = nt(d_mlp, down_buf[8 * half : 8 * half + 8].reshape(C, C))
        dact[half] = value.astype(BF).astype(F32)

    def hidden_cot(half):
        for image in range(2):
            factor = dact[half, image : image + 1, :]

            def rows_cot(index, carry):
                rows = pl.ds(pl.multiple_of(image * 256 + index * 16, 16), 16)
                dhid[half, rows, :] = (gprime[half, rows, :] * factor).astype(BF)
                return carry

            lax.fori_loop(0, 16, rows_cot, 0)

    def up_grad_half(half):
        hidden_cot(half)
        g_buf[half] = tn(normed[...], dhid[half]).astype(BF).reshape(16, 48, C)

    up_grad_half(1 - core)
    r1 = []
    for part in range(2):
        chips = pl.ds(8 * part, 8)
        copy = remote(
            g_buf.at[1 - core, chips],
            rs1.at[chips],
            r1_send.at[part],
            r1_recv.at[part],
            me_loop,
            sib_dp,
        )
        send(copy)
        r1.append(copy)
    up_grad_half(core)
    for copy in r1:
        copy.wait_recv()

    def core_sum(where):
        s1[where] = (g_buf[core, where].astype(F32) + rs1[where].astype(F32)).astype(BF)

    def x_copy(z):
        where = z * 2 + 1 - xlo
        target = me_loop + lax.rem(z, 2) * (loop_b - me_loop)
        return remote(s1.at[where], rs2.at[z], r2_send.at[z], r2_recv.at[z], target, xnb_dp)

    @pl.loop(1, N_Z + 1)
    def _(o):
        z = lax.rem(zed + o, N_Z)
        core_sum(z * 2 + 1 - xlo)
        x_copy(z).start()

    @pl.loop(0, N_Z)
    def _(z):
        core_sum(z * 2 + xlo)

    hid[...] = nt(dhid[0], up_buf[0].reshape(C, C)) + nt(dhid[1], up_buf[1].reshape(C, C))

    dpad = conv_pad
    for image in range(2):
        for j in (0, 1, 2, 19, 20, 21, 22):
            dpad[image, j] = jnp.zeros((16, C), F32)

    def norm_cot(index, carry):
        rows = pl.ds(pl.multiple_of(index * 16, 16), 16)
        d_hat = hid[rows, :].astype(BF).astype(F32) * gain_row
        hat = xhat[rows, :]
        first = jnp.mean(d_hat, axis=-1, keepdims=True)
        second = jnp.mean(d_hat * hat, axis=-1, keepdims=True)
        dpad[index // 16, lax.rem(index, 16) + 3] = rstd[rows, :1] * (
            d_hat - first - hat * second
        )
        return carry

    lax.fori_loop(0, 32, norm_cot, 0)

    def z_copy(o):
        z = lax.rem(zed + o, N_Z)
        return remote(
            s2.at[z],
            rs3.at[o - 1],
            r3_send.at[o - 1],
            r3_recv.at[o - 1],
            me_loop,
            z * 4 + xlo * 2 + core,
        )

    def x_sum(z):
        x_copy(z).wait_recv()
        s2[z] = (s1[z * 2 + xlo].astype(F32) + rs2[z].astype(F32)).astype(BF)

    @pl.loop(1, N_Z)
    def _(o):
        x_sum(lax.rem(zed + o, N_Z))
        z_copy(o).start()

    x_sum(zed)

    kg[...] = jnp.zeros(kg.shape, F32)

    def slab_copy(slab):
        return remote(
            kg.at[slab], kr1.at[me_dp], p1_send.at[slab], p1_recv.at[me_dp], me_loop, slab
        )

    tap_at = lax.broadcasted_iota(jnp.int32, (8, 128), 0)

    def kernel_chunk(cb, offset):
        lanes = chunk_lanes(cb)

        def column(b, carry):
            accs = [jnp.zeros((2, 8, 128), F32) for _ in range(7)]
            for image in range(2):

                def row(r, state):
                    view = shifted[image * 6 + cb, b, r].reshape(2, 8, 128)
                    window = state[0]
                    accs = [state[1][a] + view * window[6 - a] for a in range(7)]
                    ahead = dpad[image, r + 7, :, lanes].reshape(2, 8, 128)
                    return (window[1:] + (ahead,), tuple(accs))

                window = tuple(
                    dpad[image, j, :, lanes].reshape(2, 8, 128) for j in range(7)
                )
                _, accs = lax.fori_loop(0, 16, row, (window, tuple(accs)))
            slab0 = (cb // 2) * 7
            for a in range(7):
                value = jnp.sum(accs[a][0] + accs[a][1], axis=0, keepdims=True)
                columns = slice(offset, offset + 128)
                kg[slab0 + a, :, columns] = kg[slab0 + a, :, columns] + jnp.where(
                    tap_at == b, value, 0.0
                )
            return carry

        lax.fori_loop(0, 7, column, 0)

    for group in range(3):
        kernel_chunk(2 * group, 0)
        kernel_chunk(2 * group + 1, 128)
        for a in range(7):
            slab = group * 7 + a

            @pl.when(me_dp != slab)
            def _():
                slab_copy(slab).start()

    total = s2[zed].astype(F32)
    for o in range(1, N_Z):
        z_copy(o).wait_recv()
        total = total + rs3[o - 1].astype(F32)
    for q in range(N_PIECE):
        rb, lh = q // 2, q % 2
        p3[q] = total[rb * 8 : rb * 8 + 8, lh * 384 : lh * 384 + 384]

    def piece_copy(q):
        return remote(p3.at[q], rs4.at[me_loop], r4_send.at[q], r4_recv.at[me_loop], q, me_dp)

    for q in range(N_PIECE):

        @pl.when(me_loop != q)
        def _():
            piece_copy(q).start()

    def p1_wait(o):
        other = lax.rem(me_dp + o, N_DP)
        remote(
            kr1.at[other], kr1.at[other], p1_send.at[0], p1_recv.at[other], me_loop, sib_dp
        ).wait_recv()
        return other

    def share_copy(o):
        return remote(
            kr2.at[me_loop],
            kr2.at[me_loop],
            p2_send.at[o],
            p2_recv.at[o],
            lax.rem(me_loop + o, N_LOOP),
            me_dp,
        )

    @pl.when(me_dp < N_SLAB)
    def _():
        k1[...] = kg[me_dp]

        @pl.loop(1, N_DP)
        def _(o):
            other = p1_wait(o)
            k1[...] = k1[...] + kr1[other]

        kr2[me_loop] = k1[...]

        @pl.loop(1, N_LOOP)
        def _(o):
            share_copy(o).start()

    target_core = me_loop // 6
    target_dp = chip * 2 + target_core
    own_piece = lax.rem(me_loop, 6)

    def result_copy(o):
        return remote(
            r4,
            fin.at[core, own_piece],
            r5_send.at[o],
            r5_recv.at[core, own_piece],
            lax.rem(me_loop + o, N_LOOP),
            target_dp,
        )

    @pl.when(me_loop < N_PIECE)
    def _():
        r4[...] = p3[me_loop]

        @pl.loop(1, N_LOOP)
        def _(o):
            other = lax.rem(me_loop + o, N_LOOP)
            remote(
                rs4.at[other], rs4.at[other], r4_send.at[0], r4_recv.at[other], me_loop, sib_dp
            ).wait_recv()
            r4[...] = r4[...] + rs4[other]

        @pl.loop(1, N_LOOP)
        def _(o):
            result_copy(o).start()

        @pl.when(target_core != core)
        def _():
            remote(
                r4,
                fin.at[core, own_piece],
                r5_send.at[0],
                r5_recv.at[core, own_piece],
                me_loop,
                sib_dp,
            ).start()

        @pl.when(target_core == core)
        def _():
            fin[core, own_piece] = r4[...]

    def spread_copy(o):
        return remote(
            k1,
            kfin.at[me_dp],
            p3_send.at[o],
            p3_recv.at[me_dp],
            me_loop,
            lax.rem(me_dp + o, N_DP),
        )

    @pl.when(me_dp < N_SLAB)
    def _():
        @pl.loop(1, N_LOOP)
        def _(o):
            share_copy(o).wait_recv()

        summed = kr2[0]
        for l in range(1, N_LOOP):
            summed = summed + kr2[l]
        k1[...] = summed

        @pl.loop(1, N_DP)
        def _(o):
            spread_copy(o).start()

        kfin[me_dp] = summed

    @pl.loop(1, N_LOOP)
    def _(o):
        msg_copy(o).wait_recv()

    for l in range(N_LOOP):
        msg_all[2 * l : 2 * l + 2, :] = msg_buf[l]
    all_emb = msg_all[:, :E]
    all_weight = msg_all[:, E:]
    pick_row = lax.broadcasted_iota(jnp.int32, (8, 128), 0)
    pick_col = lax.broadcasted_iota(jnp.int32, (8, 128), 1)
    pick = jnp.where((pick_col == 2 * me_loop + pick_row) & (pick_row < 2), 1.0, 0.0)
    mine = nt(pick, all_weight, HI)
    text_cot = logit_scale * jnp.dot(mine, all_emb, precision=HI, preferred_element_type=F32)
    text_cot = text_cot[:2]
    own_rows = text[...].astype(F32)
    own_norm = jnp.sqrt(jnp.sum(own_rows * own_rows, axis=-1, keepdims=True) + EPS)
    own_hat = own_rows / own_norm
    text_out[...] = (
        text_cot - own_hat * jnp.sum(own_hat * text_cot, axis=-1, keepdims=True)
    ) / own_norm

    for cs in range(2):
        for j in range(6):

            @pl.when((core * 6 + j != me_loop) | (core != cs))
            def _():
                remote(
                    r4, fin.at[cs, j], r5_send.at[0], r5_recv.at[cs, j], me_loop, sib_dp
                ).wait_recv()

            rb, lh = j // 2, j % 2
            up_out[rb * 8 : rb * 8 + 8, cs * C + lh * 384 : cs * C + lh * 384 + 384] = fin[cs, j]

    for slab in range(N_SLAB):

        @pl.when(me_dp != slab)
        def _():
            remote(
                k1, kfin.at[slab], p3_send.at[0], p3_recv.at[slab], me_loop, sib_dp
            ).wait_recv()

        lp, a = slab // 7, slab % 7
        kernel_out[a, :, lp * 256 : lp * 256 + 256] = kfin[slab, :7]

    for copy in pending:
        copy.wait_send()
    for copy in pre:
        copy.wait_send()

    @pl.loop(1, N_LOOP)
    def _(o):
        text_copy(o).wait_send()
        msg_copy(o).wait_send()

    @pl.loop(0, N_Z)
    def _(z):
        x_copy(z).wait_send()

    @pl.loop(1, N_Z)
    def _(o):
        z_copy(o).wait_send()

    for slab in range(N_SLAB):

        @pl.when(me_dp != slab)
        def _():
            slab_copy(slab).wait_send()

    for q in range(N_PIECE):

        @pl.when(me_loop != q)
        def _():
            piece_copy(q).wait_send()

    @pl.when(me_loop < N_PIECE)
    def _():
        @pl.loop(1, N_LOOP)
        def _(o):
            result_copy(o).wait_send()

        @pl.when(target_core != core)
        def _():
            result_copy(0).wait_send()

    @pl.when(me_dp < N_SLAB)
    def _():
        @pl.loop(1, N_LOOP)
        def _(o):
            share_copy(o).wait_send()

        @pl.loop(1, N_DP)
        def _(o):
            spread_copy(o).wait_send()


def body(
    images,
    kernel,
    ln_gain,
    w_up,
    b_up,
    w_down,
    layer_scale,
    w_head,
    text_rows,
    pair_ids,
    log_temp,
    loss_bias,
):
    vmem = pl.BlockSpec(memory_space=pltpu.VMEM)
    smem = pl.BlockSpec(memory_space=pltpu.SMEM)
    dma = pltpu.SemaphoreType.DMA
    scratch = [
        pltpu.VMEM((2, 2, 32, C), BF),
        pltpu.VMEM((2, 2, 32, EH), BF),
        pltpu.VMEM((2, 16, 48, C), BF),
        pltpu.VMEM((16, 2, 48, C), BF),
        pltpu.VMEM((2, 16, 48, EH), BF),
        pltpu.VMEM((N_LOOP, 2, E), F32),
        pltpu.VMEM((GROUP, E), F32),
        pltpu.VMEM((49, 8, 128), F32),
        pltpu.VMEM((12, 7, 16, 16, 128), F32),
        pltpu.VMEM((2, 23, 16, C), F32),
        pltpu.VMEM((2, 8, C), F32),
        pltpu.VMEM((512, C), BF),
        pltpu.VMEM((512, C), F32),
        pltpu.VMEM((512, 128), F32),
        pltpu.VMEM((512, C), F32),
        pltpu.VMEM((2, 512, C), F32),
        pltpu.VMEM((2, 16, C), F32),
        pltpu.VMEM((2, 512, C), BF),
        pltpu.VMEM((2, 16, 48, C), BF),
        pltpu.VMEM((16, 48, C), BF),
        pltpu.VMEM((16, 48, C), BF),
        pltpu.VMEM((8, 48, C), BF),
        pltpu.VMEM((8, 48, C), BF),
        pltpu.VMEM((7, 48, C), BF),
        pltpu.VMEM((N_PIECE, 8, 384), F32),
        pltpu.VMEM((N_LOOP, 8, 384), F32),
        pltpu.VMEM((8, 384), F32),
        pltpu.VMEM((2, 6, 8, 384), F32),
        pltpu.VMEM((N_LOOP, 2, E + 128), F32),
        pltpu.VMEM((GROUP, E + 128), F32),
        pltpu.VMEM((N_SLAB, 8, 256), F32),
        pltpu.VMEM((N_DP, 8, 256), F32),
        pltpu.VMEM((8, 256), F32),
        pltpu.VMEM((N_LOOP, 8, 256), F32),
        pltpu.VMEM((N_SLAB, 8, 256), F32),
        dma((3, 31)),
        dma((3, 31)),
        dma((2,)),
        dma((2,)),
        dma((N_LOOP,)),
        dma((N_LOOP,)),
        dma((N_LOOP,)),
        dma((N_LOOP,)),
        dma((2,)),
        dma((2,)),
        dma((N_Z,)),
        dma((N_Z,)),
        dma((N_Z,)),
        dma((N_Z,)),
        dma((N_LOOP,)),
        dma((N_LOOP,)),
        dma((N_LOOP,)),
        dma((2, 6)),
        dma((N_DP,)),
        dma((N_DP,)),
        dma((N_LOOP,)),
        dma((N_LOOP,)),
        dma((N_DP,)),
        dma((N_DP,)),
    ]
    kernel_grad, up_grad, text_grad = pl.pallas_call(
        kernel_body,
        out_shape=(
            jax.ShapeDtypeStruct((7, 7, C), F32),
            jax.ShapeDtypeStruct((24, FFW), F32),
            jax.ShapeDtypeStruct((2, E), F32),
        ),
        in_specs=[vmem] * 9 + [smem] * 3,
        out_specs=(vmem, vmem, vmem),
        scratch_shapes=scratch,
        compiler_params=pltpu.CompilerParams(
            collective_id=0, has_side_effects=True, vmem_limit_bytes=56 * 1024 * 1024
        ),
        name="tower_step",
    )(
        images[0],
        kernel,
        ln_gain.reshape(1, C),
        w_up,
        b_up.reshape(1, FFW),
        w_down,
        layer_scale.reshape(1, C),
        w_head,
        text_rows[0],
        pair_ids,
        log_temp,
        loss_bias,
    )
    return (kernel_grad, up_grad, text_grad[None])


def solution(mesh):
    placed = (
        P("dp", "loop", None, None, None),
        P(),
        P(),
        P("dp", None),
        P(),
        P("dp", None),
        P(),
        P("dp", None),
        P("dp", "loop", None),
        P("dp", "loop"),
        P(),
        P(),
    )
    return jax.shard_map(
        body,
        mesh=mesh,
        in_specs=placed,
        out_specs=(P(), P("dp", None), P("dp", "loop", None)),
        check_vma=False,
    )
```

```python
import functools

import jax
import jax.numpy as jnp
from jax import lax
from jax.experimental import pallas as pl
from jax.experimental.pallas import tpu as pltpu
from jax.sharding import PartitionSpec as P

MESH = pl.DeviceIdType.MESH
EPS = 1e-06
BF = jnp.bfloat16
F32 = jnp.float32
HI = lax.Precision.HIGHEST

N_LOOP = 16
N_DP = 32
N_Z = 8
C = 768
FFW = 1536
E = 1152
EH = 640
GROUP = 32
N_PIECE = 12
N_SLAB = 21


def nt(a, b, precision=None):
    return lax.dot_general(
        a, b, (((1,), (1,)), ((), ())), preferred_element_type=F32, precision=precision
    )


def tn(a, b):
    return lax.dot_general(a, b, (((0,), (0,)), ((), ())), preferred_element_type=F32)


def kernel_body(
    images,
    kern,
    gain,
    w_up,
    b_up,
    w_down,
    scale,
    w_head,
    text,
    pair,
    log_temp,
    loss_bias,
    kernel_out,
    up_out,
    text_out,
    pre,
    up_buf,
    mix_buf,
    text_buf,
    text_all,
    taps,
    shifted,
    conv_pad,
    img_sum,
    normed,
    xhat,
    rstd,
    hid,
    gprime,
    dact,
    dhid,
    g_buf,
    rs1,
    s1,
    rs2,
    s2,
    rs3,
    p3,
    rs4,
    r4,
    fin,
    msg_buf,
    msg_all,
    kg,
    kr1,
    k1,
    kr2,
    kfin,
    w_send,
    w_recv,
    bulk_send,
    bulk_recv,
    z_send,
    x_send,
    y_send,
    y_recv,
    pre_sem,
    text_sem,
    msg_sem,
    r1_sem,
    r2_send,
    r2_recv,
    r3_sem,
    r4_sem,
    r5_sem,
    p1_sem,
    p2_sem,
    p3_sem,
):
    me_loop = lax.axis_index("loop")
    me_dp = lax.axis_index("dp")
    core = lax.rem(me_dp, 2)
    xlo = lax.rem(me_dp // 2, 2)
    zed = me_dp // 4
    chip = me_dp // 2
    xhi = lax.rem(me_loop, 2)
    sib_dp = me_dp + 1 - 2 * core
    xnb_dp = me_dp + 2 - 4 * xlo
    loop_b = me_loop + 1 - 2 * xhi
    sgn = 1 - 2 * core

    def z_dp(offset):
        return lax.rem(zed + offset + N_Z, N_Z) * 4 + xlo * 2 + core

    def remote(src, dst, send, recv, loop, dp):
        return pltpu.make_async_remote_copy(
            src_ref=src,
            dst_ref=dst,
            send_sem=send,
            recv_sem=recv,
            device_id=(loop, dp),
            device_id_type=MESH,
        )

    barrier = pltpu.get_barrier_semaphore()

    @pl.loop(1, N_DP)
    def _(o):
        pl.semaphore_signal(
            barrier, inc=1, device_id=(me_loop, lax.rem(me_dp + o, N_DP)), device_id_type=MESH
        )

    @pl.loop(1, N_LOOP)
    def _(o):
        other = lax.rem(me_loop + o, N_LOOP)
        pl.semaphore_signal(barrier, inc=1, device_id=(other, me_dp), device_id_type=MESH)
        pl.semaphore_signal(barrier, inc=1, device_id=(other, sib_dp), device_id_type=MESH)

    pl.semaphore_signal(barrier, inc=1, device_id=(loop_b, xnb_dp), device_id_type=MESH)

    zero8 = jnp.zeros((8, C), F32)
    for half in range(2):
        rows = w_up[:, half * C : (half + 1) * C].astype(F32)
        pre[0, half, 0] = jnp.concatenate([rows, zero8], axis=0).astype(BF)
        rows = w_head[:, half * EH : min((half + 1) * EH, E)].astype(F32)
        rows = jnp.concatenate([rows, jnp.zeros((24, C - rows.shape[1]), F32)], axis=1)
        pre[0, half, 1] = jnp.concatenate([rows, zero8], axis=0).astype(BF)
    text_buf[me_loop] = text[...].astype(F32)

    pl.semaphore_wait(barrier, N_DP - 1 + 2 * (N_LOOP - 1) + 1)

    def whole(ref, sem, recv_sem=None):
        return remote(ref, ref, sem, sem if recv_sem is None else recv_sem, me_loop, sib_dp)

    parity = lax.rem(me_loop // 2, 2)
    mix_of = (0, parity, 1 - parity)

    def slab_of(w, owner_core, where):
        if w == 0:
            return up_buf.at[owner_core, where]
        return mix_buf.at[mix_of[w], where, owner_core]

    def to_sibling(w, where):
        slab = slab_of(w, core, where)
        remote(slab, slab, bulk_send.at[w], bulk_recv.at[w], me_loop, sib_dp).start()

    def to_x(w, where_z, sem):
        slab = slab_of(w, core, where_z * 2 + xlo)
        side = lax.rem(where_z, 2)
        target = me_loop + side * (loop_b - me_loop)
        remote(slab, slab, x_send.at[w], w_recv.at[w, sem], target, xnb_dp).start()

    def to_z(w, where_z, direction, sem):
        slab = slab_of(w, core, where_z * 2 + xlo)
        remote(
            slab, slab, z_send.at[w], w_recv.at[w, sem], me_loop, z_dp(direction * sgn)
        ).start()

    def to_y(where, sem):
        slab = slab_of(1, core, where)
        target = lax.rem(me_loop + 2 * sgn + N_LOOP, N_LOOP)
        remote(slab, slab, y_send, y_recv.at[sem], target, me_dp).start()

    def await_slab(w, where, sem):
        slab = slab_of(w, core, where)
        remote(slab, slab, w_send, w_recv.at[w, sem], me_loop, sib_dp).wait_recv()

    def kind_z(kind):
        offset = -kind if kind <= 4 else kind - 4
        return lax.rem(zed + offset * sgn + N_Z, N_Z)

    def begin(w):
        to_z(w, zed, 1, 0)
        to_z(w, zed, -1, 4)
        to_x(w, zed, 7)
        if w == 1:
            to_y(chip, 0)
        to_sibling(w, chip)

    def z_arrival(w, kind):
        sem = kind - 1
        where_z = kind_z(kind)
        await_slab(w, where_z * 2 + xlo, sem)
        if kind in (1, 2, 3):
            to_z(w, where_z, 1, sem + 1)
        if kind in (5, 6):
            to_z(w, where_z, -1, sem + 1)
        to_x(w, where_z, 7 + kind)
        if w == 1:
            to_y(where_z * 2 + xlo, kind)
        to_sibling(w, where_z * 2 + xlo)

    def x_arrival(w, kind):
        where = kind_z(kind) * 2 + 1 - xlo
        await_slab(w, where, 7 + kind)
        if w == 1:
            to_y(where, 8 + kind)
        to_sibling(w, where)

    def y_arrival(index):
        side = xlo if index < 8 else 1 - xlo
        where = kind_z(index % 8) * 2 + side
        slab = slab_of(2, core, where)
        remote(slab, slab, y_send, y_recv.at[index], me_loop, sib_dp).wait_recv()
        to_sibling(2, where)

    def kinds_at(step):
        z_kinds = [step] if step <= 4 else []
        z_kinds += [4 + step] if step <= 3 else []
        x_kinds = {1: [0], 5: [4]}.get(step, [step - 1, 3 + step])
        return z_kinds, x_kinds

    def turn(w, step):
        if w == 2 and step == 0:
            y_arrival(0)
            return
        z_kinds, x_kinds = kinds_at(step)
        for kind in z_kinds:
            if w == 2:
                y_arrival(kind)
            else:
                z_arrival(w, kind)
        for kind in x_kinds:
            if w == 2:
                y_arrival(8 + kind)
            else:
                x_arrival(w, kind)

    def sixteen(w):
        return up_buf.at[0] if w == 0 else mix_buf.at[0, :, 0]

    def finish(w):
        whole(sixteen(w), bulk_send.at[w], bulk_recv.at[w]).wait_recv()

    pre_copy = remote(
        pre.at[0, 1 - core], pre.at[1, 0], pre_sem.at[0], pre_sem.at[1], me_loop, sib_dp
    )
    pre_copy.start()

    def text_copy(o):
        return remote(
            text_buf.at[me_loop],
            text_buf.at[me_loop],
            text_sem.at[0],
            text_sem.at[1],
            lax.rem(me_loop + o, N_LOOP),
            me_dp,
        )

    def merge(index):
        mine = pre[0, core, index].astype(F32)[:24]
        theirs = pre[1, 0, index].astype(F32)[:24]
        first = core == 0
        joined = jnp.concatenate(
            [jnp.where(first, mine, theirs), jnp.where(first, theirs, mine)], axis=0
        )
        return joined.astype(BF)

    pre_copy.wait_recv()
    up_buf[core, chip] = merge(0)
    begin(0)
    own_mix = jnp.where(parity == 0, w_down[...].astype(F32), merge(1).astype(F32))
    mix_buf[parity, chip, core] = own_mix.astype(BF)

    @pl.loop(1, N_LOOP)
    def _(o):
        text_copy(o).start()

    width_at = lax.broadcasted_iota(jnp.int32, (16, 128), 0)

    def chunk_lanes(cb):
        return pl.ds(pl.multiple_of(cb * 128, 128), 128)

    def conv_chunk(chunk, carry):
        image, cb = chunk // 6, lax.rem(chunk, 6)
        lanes = chunk_lanes(cb)
        for a in range(7):
            for b in range(7):
                taps[a * 7 + b] = jnp.broadcast_to(kern[a, pl.ds(b, 1), lanes], (8, 128))

        def row(r, state):
            accs, total = state
            x = images[image, r, :, lanes].astype(F32)
            views = []
            for b in range(7):
                if b == 3:
                    view = x
                else:
                    view = pltpu.roll(x, (3 - b) % 16, 0)
                    inside = width_at >= 3 - b if b < 3 else width_at < 19 - b
                    view = jnp.where(inside, view, 0.0)
                shifted[chunk, b, r] = view
                views.append(view.reshape(2, 8, 128))
            fresh = []
            for j in range(7):
                acc = accs[j]
                for b in range(7):
                    acc = acc + views[b] * taps[(6 - j) * 7 + b]
                fresh.append(acc)
            conv_pad[image, r, :, lanes] = fresh[0].reshape(16, 128)
            return (tuple(fresh[1:]) + (jnp.zeros((2, 8, 128), F32),), total + views[3])

        zero = jnp.zeros((2, 8, 128), F32)
        accs, total = lax.fori_loop(0, 16, row, ((zero,) * 7, zero))
        for j in range(3):
            conv_pad[image, 16 + j, :, lanes] = accs[j].reshape(16, 128)
        img_sum[image, :, lanes] = total[0] + total[1]
        return carry

    plan = (
        ((0, 1),),
        ((0, 2), (1, 1)),
        ((0, 3), (1, 2), (2, 0)),
        ((0, 4), (1, 3), (2, 1)),
        ((0, 5), (1, 4), (2, 2)),
        ((1, 5), (2, 3)),
    )
    for group in range(6):
        lax.fori_loop(2 * group, 2 * group + 2, conv_chunk, 0)
        for w, step in plan[group]:
            turn(w, step)
        if group == 0:
            begin(1)

    gain_row = gain[...].reshape(1, C)

    def norm_rows(index, carry):
        image, r = index // 16, lax.rem(index, 16)
        rows = pl.ds(pl.multiple_of(index * 16, 16), 16)
        value = conv_pad[image, r + 3]
        centered = value - jnp.mean(value, axis=-1, keepdims=True)
        inv = lax.rsqrt(jnp.mean(centered * centered, axis=-1, keepdims=True) + EPS)
        hat = centered * inv
        xhat[rows, :] = hat
        rstd[rows, :] = jnp.broadcast_to(inv, (16, 128))
        normed[rows, :] = (hat * gain_row).astype(BF)
        return carry

    lax.fori_loop(0, 32, norm_rows, 0)
    finish(0)

    scale_row = scale[...].reshape(1, C)
    c0 = 0.7978845608028654
    row_at = lax.broadcasted_iota(jnp.int32, (16, C), 0)
    means = []
    for half in range(2):
        hid[...] = jnp.dot(
            normed[...], up_buf[half].reshape(C, C), preferred_element_type=F32
        )
        turn(2, 4 + half)
        bias = b_up[half * C : (half + 1) * C].reshape(1, C)
        image_sums = []
        for image in range(2):

            def gelu_rows(index, total):
                rows = pl.ds(pl.multiple_of(image * 256 + index * 16, 16), 16)
                h = hid[rows, :] + bias
                square = h * h
                t = jnp.tanh(c0 * h * (1.0 + 0.044715 * square))
                plus = 0.5 + 0.5 * t
                active = (h * plus).astype(BF).astype(F32)
                gprime[half, rows, :] = plus + (0.5 * c0) * h * (1.0 - t * t) * (
                    1.0 + (3 * 0.044715) * square
                )
                return total + active[:8] + active[8:]

            total = lax.fori_loop(0, 16, gelu_rows, jnp.zeros((8, C), F32))
            image_sums.append(jnp.sum(total, axis=0, keepdims=True) * (1.0 / 256))
        means.append(
            jnp.where(row_at == 0, image_sums[0], jnp.where(row_at == 1, image_sums[1], 0.0))
        )

    finish(1)
    finish(2)
    mlp = jnp.zeros((16, C), F32)
    for half in range(2):
        high = means[half].astype(BF)
        low = (means[half] - high.astype(F32)).astype(BF)
        rows = mix_buf[0, 8 * half : 8 * half + 8].reshape(C, C)
        mlp = mlp + jnp.dot(high, rows, preferred_element_type=F32)
        mlp = mlp + jnp.dot(low, rows, preferred_element_type=F32)
    img_mean = [jnp.sum(img_sum[image], axis=0, keepdims=True) * (1.0 / 256) for image in range(2)]
    img_mean = jnp.where(row_at == 0, img_mean[0], jnp.where(row_at == 1, img_mean[1], 0.0))
    pooled = (img_mean + scale_row * mlp).astype(BF)
    raw = [
        jnp.dot(
            pooled, mix_buf[1, :, half, :, :EH].reshape(C, EH), preferred_element_type=F32
        )
        for half in range(2)
    ]
    norm = lax.rsqrt(
        jnp.sum(raw[0] * raw[0], axis=-1, keepdims=True)
        + jnp.sum(raw[1] * raw[1], axis=-1, keepdims=True)
        + EPS
    )
    emb = jnp.concatenate([raw[0] * norm, raw[1][:, : E - EH] * norm], axis=1)

    whole(text_buf.at[pl.ds(0, N_LOOP - 1)], text_sem.at[0], text_sem.at[1]).wait_recv()
    for l in range(N_LOOP):
        text_all[2 * l : 2 * l + 2, :] = text_buf[l]
    raw_rows = text_all[...]
    text_norm = jnp.sqrt(jnp.sum(raw_rows * raw_rows, axis=-1, keepdims=True) + EPS)
    text_emb = (raw_rows / text_norm).astype(BF).astype(F32)
    logit_scale = jnp.exp(jnp.full((1, 1), log_temp[0], F32))
    logits = logit_scale * nt(emb, text_emb, HI) + loss_bias[0]
    pair_row_at = lax.broadcasted_iota(jnp.int32, (16, GROUP), 0)
    pair_col_at = lax.broadcasted_iota(jnp.int32, (16, GROUP), 1)
    own = jnp.where(pair_row_at == 0, pair[0, 0], pair[0, 1])
    signs = jnp.where(own == pair_col_at, 1.0, -1.0)
    weight = -signs * jax.nn.sigmoid(-signs * logits) / GROUP
    weight = jnp.where(pair_row_at < 2, weight, 0.0)
    image_cot = logit_scale * jnp.dot(weight, text_emb, precision=HI, preferred_element_type=F32)

    msg_buf[me_loop, :, :E] = emb[:2]
    msg_buf[me_loop, :, E:] = jnp.concatenate(
        [weight[:2], jnp.zeros((2, 128 - GROUP), F32)], axis=1
    )

    def msg_copy(o):
        return remote(
            msg_buf.at[me_loop],
            msg_buf.at[me_loop],
            msg_sem.at[0],
            msg_sem.at[1],
            lax.rem(me_loop + o, N_LOOP),
            me_dp,
        )

    d_raw = norm * (image_cot - emb * jnp.sum(image_cot * emb, axis=-1, keepdims=True))
    d_raw = d_raw.astype(BF)
    d_pooled = nt(d_raw[:, :EH], mix_buf[1, :, 0, :, :EH].reshape(C, EH)) + nt(
        d_raw[:, EH:], mix_buf[1, :, 1, :, : E - EH].reshape(C, E - EH)
    )
    d_pooled = d_pooled.astype(BF).astype(F32)
    d_mlp = (scale_row * (d_pooled * (1.0 / 256))).astype(BF)
    for half in range(2):
        value = nt(d_mlp, mix_buf[0, 8 * half : 8 * half + 8].reshape(C, C))
        dact[half] = value.astype(BF).astype(F32)

    def hidden_cot(half):
        for image in range(2):
            factor = dact[half, image : image + 1, :]

            def rows_cot(index, carry):
                rows = pl.ds(pl.multiple_of(image * 256 + index * 16, 16), 16)
                dhid[half, rows, :] = (gprime[half, rows, :] * factor).astype(BF)
                return carry

            lax.fori_loop(0, 16, rows_cot, 0)

    def up_grad_half(half):
        hidden_cot(half)
        g_buf[half] = tn(normed[...], dhid[half]).astype(BF).reshape(16, 48, C)

    up_grad_half(1 - core)
    r1 = remote(g_buf.at[1 - core], rs1, r1_sem.at[0], r1_sem.at[1], me_loop, sib_dp)
    r1.start()
    up_grad_half(core)
    r1.wait_recv()

    def core_sum(where):
        s1[where] = (g_buf[core, where].astype(F32) + rs1[where].astype(F32)).astype(BF)

    def x_copy(z):
        where = z * 2 + 1 - xlo
        target = me_loop + lax.rem(z, 2) * (loop_b - me_loop)
        return remote(s1.at[where], rs2.at[z], r2_send, r2_recv.at[z], target, xnb_dp)

    @pl.loop(1, N_Z + 1)
    def _(o):
        z = lax.rem(zed + o, N_Z)
        core_sum(z * 2 + 1 - xlo)
        x_copy(z).start()

    @pl.loop(0, N_Z)
    def _(z):
        core_sum(z * 2 + xlo)

    @pl.loop(1, N_LOOP)
    def _(o):
        msg_copy(o).start()

    hid[...] = nt(dhid[0], up_buf[0].reshape(C, C)) + nt(dhid[1], up_buf[1].reshape(C, C))

    dconv = conv_pad

    def norm_cot(index, carry):
        rows = pl.ds(pl.multiple_of(index * 16, 16), 16)
        d_hat = hid[rows, :].astype(BF).astype(F32) * gain_row
        hat = xhat[rows, :]
        first = jnp.mean(d_hat, axis=-1, keepdims=True)
        second = jnp.mean(d_hat * hat, axis=-1, keepdims=True)
        dconv[index // 16, lax.rem(index, 16)] = rstd[rows, :1] * (
            d_hat - first - hat * second
        )
        return carry

    lax.fori_loop(0, 32, norm_cot, 0)

    def z_copy(o):
        z = lax.rem(zed + o, N_Z)
        return remote(
            s2.at[z],
            rs3.at[o - 1],
            r3_sem.at[0],
            r3_sem.at[1],
            me_loop,
            z * 4 + xlo * 2 + core,
        )

    def x_sum(z):
        x_copy(z).wait_recv()
        s2[z] = (s1[z * 2 + xlo].astype(F32) + rs2[z].astype(F32)).astype(BF)

    @pl.loop(1, N_Z)
    def _(o):
        x_sum(lax.rem(zed + o, N_Z))
        z_copy(o).start()

    x_sum(zed)

    kg[...] = jnp.zeros(kg.shape, F32)

    def slab_copy(slab):
        return remote(
            kg.at[slab], kr1.at[me_dp], p1_sem.at[0], p1_sem.at[1], me_loop, slab
        )

    tap_at = lax.broadcasted_iota(jnp.int32, (8, 128), 0)

    def kernel_chunk(cb, offset):
        lanes = chunk_lanes(cb)

        def column(b, carry):
            accs = [jnp.zeros((2, 8, 128), F32) for _ in range(7)]
            for image in range(2):
                window = {}
                for r in range(16):
                    view = shifted[image * 6 + cb, b, r].reshape(2, 8, 128)
                    for a in range(7):
                        h = r - a + 3
                        if 0 <= h < 16:
                            if h not in window:
                                value = dconv[image, h, :, lanes]
                                window[h] = value.reshape(2, 8, 128)
                            accs[a] = accs[a] + view * window[h]
            slab0 = (cb // 2) * 7
            for a in range(7):
                value = jnp.sum(accs[a][0] + accs[a][1], axis=0, keepdims=True)
                columns = slice(offset, offset + 128)
                kg[slab0 + a, :, columns] = kg[slab0 + a, :, columns] + jnp.where(
                    tap_at == b, value, 0.0
                )
            return carry

        lax.fori_loop(0, 7, column, 0)

    for group in range(3):
        kernel_chunk(2 * group, 0)
        kernel_chunk(2 * group + 1, 128)
        for a in range(7):
            slab = group * 7 + a

            @pl.when(me_dp != slab)
            def _():
                slab_copy(slab).start()

    whole(msg_buf.at[pl.ds(0, N_LOOP - 1)], msg_sem.at[0], msg_sem.at[1]).wait_recv()
    for l in range(N_LOOP):
        msg_all[2 * l : 2 * l + 2, :] = msg_buf[l]
    all_emb = msg_all[:, :E]
    all_weight = msg_all[:, E:]
    pick_row = lax.broadcasted_iota(jnp.int32, (8, 128), 0)
    pick_col = lax.broadcasted_iota(jnp.int32, (8, 128), 1)
    pick = jnp.where((pick_col == 2 * me_loop + pick_row) & (pick_row < 2), 1.0, 0.0)
    mine = nt(pick, all_weight, HI)
    text_cot = logit_scale * jnp.dot(mine, all_emb, precision=HI, preferred_element_type=F32)
    text_cot = text_cot[:2]
    own_rows = text[...].astype(F32)
    own_norm = jnp.sqrt(jnp.sum(own_rows * own_rows, axis=-1, keepdims=True) + EPS)
    own_hat = own_rows / own_norm
    text_out[...] = (
        text_cot - own_hat * jnp.sum(own_hat * text_cot, axis=-1, keepdims=True)
    ) / own_norm

    def share_copy(o):
        return remote(
            kr2.at[me_loop],
            kr2.at[me_loop],
            p2_sem.at[0],
            p2_sem.at[1],
            lax.rem(me_loop + o, N_LOOP),
            me_dp,
        )

    @pl.when(me_dp < N_SLAB)
    def _():
        whole(kr1.at[pl.ds(0, N_DP - 1)], p1_sem.at[0], p1_sem.at[1]).wait_recv()
        kr1[me_dp] = kg[me_dp]
        summed = kr1[0]
        for d in range(1, N_DP):
            summed = summed + kr1[d]
        kr2[me_loop] = summed

        @pl.loop(1, N_LOOP)
        def _(o):
            share_copy(o).start()

    total = s2[zed].astype(F32)
    whole(rs3, r3_sem.at[0], r3_sem.at[1]).wait_recv()
    for o in range(1, N_Z):
        total = total + rs3[o - 1].astype(F32)
    for q in range(N_PIECE):
        rb, lh = q // 2, q % 2
        p3[q] = total[rb * 8 : rb * 8 + 8, lh * 384 : lh * 384 + 384]

    def piece_copy(q):
        return remote(p3.at[q], rs4.at[me_loop], r4_sem.at[0], r4_sem.at[1], q, me_dp)

    for q in range(N_PIECE):

        @pl.when(me_loop != q)
        def _():
            piece_copy(q).start()

    def spread_copy(o):
        return remote(
            k1,
            kfin.at[me_dp],
            p3_sem.at[0],
            p3_sem.at[1],
            me_loop,
            lax.rem(me_dp + o, N_DP),
        )

    @pl.when(me_dp < N_SLAB)
    def _():
        whole(kr2.at[pl.ds(0, N_LOOP - 1)], p2_sem.at[0], p2_sem.at[1]).wait_recv()
        summed = kr2[0]
        for l in range(1, N_LOOP):
            summed = summed + kr2[l]
        k1[...] = summed

        @pl.loop(1, N_DP)
        def _(o):
            spread_copy(o).start()

        kfin[me_dp] = summed

    target_core = me_loop // 6
    target_dp = chip * 2 + target_core
    own_piece = lax.rem(me_loop, 6)

    def result_copy(o):
        return remote(
            r4,
            fin.at[core * 6 + own_piece],
            r5_sem.at[0],
            r5_sem.at[1],
            lax.rem(me_loop + o, N_LOOP),
            target_dp,
        )

    @pl.when(me_loop < N_PIECE)
    def _():
        whole(rs4.at[pl.ds(0, N_LOOP - 1)], r4_sem.at[0], r4_sem.at[1]).wait_recv()
        rs4[me_loop] = p3[me_loop]
        summed = rs4[0]
        for l in range(1, N_LOOP):
            summed = summed + rs4[l]
        r4[...] = summed

        @pl.loop(1, N_LOOP)
        def _(o):
            result_copy(o).start()

        @pl.when(target_core != core)
        def _():
            remote(
                r4,
                fin.at[core * 6 + own_piece],
                r5_sem.at[0],
                r5_sem.at[1],
                me_loop,
                sib_dp,
            ).start()

        @pl.when(target_core == core)
        def _():
            fin[core * 6 + own_piece] = r4[...]

    own_result = (target_core == core) & (me_loop < N_PIECE)

    @pl.when(own_result)
    def _():
        whole(fin.at[pl.ds(0, N_PIECE - 1)], r5_sem.at[0], r5_sem.at[1]).wait_recv()

    @pl.when(jnp.logical_not(own_result))
    def _():
        whole(fin, r5_sem.at[0], r5_sem.at[1]).wait_recv()

    for cs in range(2):
        for j in range(6):
            rb, lh = j // 2, j % 2
            columns = slice(cs * C + lh * 384, cs * C + lh * 384 + 384)
            up_out[rb * 8 : rb * 8 + 8, columns] = fin[cs * 6 + j]

    @pl.when(me_dp < N_SLAB)
    def _():
        some = pl.ds(0, N_SLAB - 1)
        whole(kfin.at[some], p3_sem.at[0], p3_sem.at[1]).wait_recv()
        whole(kg.at[some], p1_sem.at[0]).wait_send()
        whole(kr2.at[pl.ds(0, N_LOOP - 1)], p2_sem.at[0]).wait_send()
        whole(kr1.at[pl.ds(0, N_DP - 1)], p3_sem.at[0]).wait_send()

    @pl.when(me_dp >= N_SLAB)
    def _():
        whole(kfin, p3_sem.at[0], p3_sem.at[1]).wait_recv()
        whole(kg, p1_sem.at[0]).wait_send()

    for slab in range(N_SLAB):
        lp, a = slab // 7, slab % 7
        kernel_out[a, :, lp * 256 : lp * 256 + 256] = kfin[slab, :7]

    pre_copy.wait_send()
    for w in range(3):
        whole(sixteen(w), bulk_send.at[w]).wait_send()
    for w in range(2):
        whole(up_buf.at[0, pl.ds(0, 7)], z_send.at[w]).wait_send()
        whole(up_buf.at[0, pl.ds(0, 8)], x_send.at[w]).wait_send()
    whole(sixteen(0), y_send).wait_send()
    whole(text_buf.at[pl.ds(0, N_LOOP - 1)], text_sem.at[0]).wait_send()
    whole(msg_buf.at[pl.ds(0, N_LOOP - 1)], msg_sem.at[0]).wait_send()
    r1.wait_send()
    whole(rs2, r2_send).wait_send()
    whole(rs3, r3_sem.at[0]).wait_send()

    @pl.when(me_loop < N_PIECE)
    def _():
        whole(p3.at[pl.ds(0, N_PIECE - 1)], r4_sem.at[0]).wait_send()

        @pl.when(target_core != core)
        def _():
            whole(rs4, r5_sem.at[0]).wait_send()

        @pl.when(target_core == core)
        def _():
            whole(rs4.at[pl.ds(0, N_LOOP - 1)], r5_sem.at[0]).wait_send()

    @pl.when(me_loop >= N_PIECE)
    def _():
        whole(p3, r4_sem.at[0]).wait_send()


def body(
    images,
    kernel,
    ln_gain,
    w_up,
    b_up,
    w_down,
    layer_scale,
    w_head,
    text_rows,
    pair_ids,
    log_temp,
    loss_bias,
):
    vmem = pl.BlockSpec(memory_space=pltpu.VMEM)
    smem = pl.BlockSpec(memory_space=pltpu.SMEM)
    dma = pltpu.SemaphoreType.DMA
    scratch = [
        pltpu.VMEM((2, 2, 2, 32, C), BF),
        pltpu.VMEM((2, 16, 48, C), BF),
        pltpu.VMEM((2, 16, 2, 48, C), BF),
        pltpu.VMEM((N_LOOP, 2, E), F32),
        pltpu.VMEM((GROUP, E), F32),
        pltpu.VMEM((49, 8, 128), F32),
        pltpu.VMEM((12, 7, 16, 16, 128), F32),
        pltpu.VMEM((2, 19, 16, C), F32),
        pltpu.VMEM((2, 8, C), F32),
        pltpu.VMEM((512, C), BF),
        pltpu.VMEM((512, C), F32),
        pltpu.VMEM((512, 128), F32),
        pltpu.VMEM((512, C), F32),
        pltpu.VMEM((2, 512, C), F32),
        pltpu.VMEM((2, 16, C), F32),
        pltpu.VMEM((2, 512, C), BF),
        pltpu.VMEM((2, 16, 48, C), BF),
        pltpu.VMEM((16, 48, C), BF),
        pltpu.VMEM((16, 48, C), BF),
        pltpu.VMEM((8, 48, C), BF),
        pltpu.VMEM((8, 48, C), BF),
        pltpu.VMEM((7, 48, C), BF),
        pltpu.VMEM((N_PIECE, 8, 384), F32),
        pltpu.VMEM((N_LOOP, 8, 384), F32),
        pltpu.VMEM((8, 384), F32),
        pltpu.VMEM((N_PIECE, 8, 384), F32),
        pltpu.VMEM((N_LOOP, 2, E + 128), F32),
        pltpu.VMEM((GROUP, E + 128), F32),
        pltpu.VMEM((N_SLAB, 8, 256), F32),
        pltpu.VMEM((N_DP, 8, 256), F32),
        pltpu.VMEM((8, 256), F32),
        pltpu.VMEM((N_LOOP, 8, 256), F32),
        pltpu.VMEM((N_SLAB, 8, 256), F32),
        dma,
        dma((2, 15)),
        dma((3,)),
        dma((3,)),
        dma((2,)),
        dma((2,)),
        dma,
        dma((16,)),
        dma((2,)),
        dma((2,)),
        dma((2,)),
        dma((2,)),
        dma,
        dma((N_Z,)),
        dma((2,)),
        dma((2,)),
        dma((2,)),
        dma((2,)),
        dma((2,)),
        dma((2,)),
    ]
    kernel_grad, up_grad, text_grad = pl.pallas_call(
        kernel_body,
        out_shape=(
            jax.ShapeDtypeStruct((7, 7, C), F32),
            jax.ShapeDtypeStruct((24, FFW), F32),
            jax.ShapeDtypeStruct((2, E), F32),
        ),
        in_specs=[vmem] * 9 + [smem] * 3,
        out_specs=(vmem, vmem, vmem),
        scratch_shapes=scratch,
        compiler_params=pltpu.CompilerParams(
            collective_id=0, has_side_effects=True, vmem_limit_bytes=56 * 1024 * 1024
        ),
        name="tower_step",
    )(
        images[0],
        kernel,
        ln_gain,
        w_up,
        b_up,
        w_down,
        layer_scale,
        w_head,
        text_rows[0],
        pair_ids,
        log_temp,
        loss_bias,
    )
    return (kernel_grad, up_grad, text_grad[None])


def solution(mesh):
    placed = (
        P("dp", "loop", None, None, None),
        P(),
        P(),
        P("dp", None),
        P(),
        P("dp", None),
        P(),
        P("dp", None),
        P("dp", "loop", None),
        P("dp", "loop"),
        P(),
        P(),
    )
    return jax.shard_map(
        body,
        mesh=mesh,
        in_specs=placed,
        out_specs=(P(), P("dp", None), P("dp", "loop", None)),
        check_vma=False,
    )
```

```python
import functools

import jax
import jax.numpy as jnp
from jax import lax
from jax.experimental import pallas as pl
from jax.experimental.pallas import tpu as pltpu
from jax.sharding import PartitionSpec as P

MESH = pl.DeviceIdType.MESH
EPS = 1e-06
BF = jnp.bfloat16
F32 = jnp.float32
HI = lax.Precision.HIGHEST

N_LOOP = 16
N_DP = 32
N_Z = 8
C = 768
FFW = 1536
E = 1152
EH = 640
GROUP = 32
N_PIECE = 12
N_SLAB = 12


def nt(a, b, precision=None):
    return lax.dot_general(
        a, b, (((1,), (1,)), ((), ())), preferred_element_type=F32, precision=precision
    )


def tn(a, b):
    return lax.dot_general(a, b, (((0,), (0,)), ((), ())), preferred_element_type=F32)


def kernel_body(
    images,
    kern,
    gain,
    w_up,
    b_up,
    w_down,
    scale,
    w_head,
    text,
    pair,
    log_temp,
    loss_bias,
    kernel_out,
    up_out,
    text_out,
    pre,
    up_buf,
    mix_buf,
    text_buf,
    text_all,
    taps,
    shifted,
    conv_pad,
    img_sum,
    normed,
    xhat,
    rstd,
    hid,
    gprime,
    dact,
    dhid,
    g_buf,
    rs1,
    s1,
    rs2,
    s2,
    rs3,
    p3,
    rs4,
    r4,
    fin,
    msg_buf,
    msg_all,
    kg,
    kg_out,
    kr1,
    k1,
    kr2,
    kfin,
    w_send,
    w_recv,
    bulk_send,
    bulk_recv,
    z_send,
    x_send,
    y_send,
    y_recv,
    pre_sem,
    text_sem,
    msg_sem,
    r1_sem,
    r2_send,
    r2_recv,
    r3_sem,
    r4_sem,
    r5_sem,
    p1_sem,
    p2_sem,
    p3_sem,
):
    me_loop = lax.axis_index("loop")
    me_dp = lax.axis_index("dp")
    core = lax.rem(me_dp, 2)
    xlo = lax.rem(me_dp // 2, 2)
    zed = me_dp // 4
    chip = me_dp // 2
    xhi = lax.rem(me_loop, 2)
    sib_dp = me_dp + 1 - 2 * core
    xnb_dp = me_dp + 2 - 4 * xlo
    loop_b = me_loop + 1 - 2 * xhi
    sgn = 1 - 2 * core

    def z_dp(offset):
        return lax.rem(zed + offset + N_Z, N_Z) * 4 + xlo * 2 + core

    def remote(src, dst, send, recv, loop, dp):
        return pltpu.make_async_remote_copy(
            src_ref=src,
            dst_ref=dst,
            send_sem=send,
            recv_sem=recv,
            device_id=(loop, dp),
            device_id_type=MESH,
        )

    barrier = pltpu.get_barrier_semaphore()

    @pl.loop(1, N_DP)
    def _(o):
        pl.semaphore_signal(
            barrier, inc=1, device_id=(me_loop, lax.rem(me_dp + o, N_DP)), device_id_type=MESH
        )

    @pl.loop(1, N_LOOP)
    def _(o):
        other = lax.rem(me_loop + o, N_LOOP)
        pl.semaphore_signal(barrier, inc=1, device_id=(other, me_dp), device_id_type=MESH)
        pl.semaphore_signal(barrier, inc=1, device_id=(other, sib_dp), device_id_type=MESH)

    pl.semaphore_signal(barrier, inc=1, device_id=(loop_b, xnb_dp), device_id_type=MESH)

    zero8 = jnp.zeros((8, C), F32)
    for half in range(2):
        rows = w_up[:, half * C : (half + 1) * C].astype(F32)
        pre[0, half, 0] = jnp.concatenate([rows, zero8], axis=0).astype(BF)
        rows = w_head[:, half * EH : min((half + 1) * EH, E)].astype(F32)
        rows = jnp.concatenate([rows, jnp.zeros((24, C - rows.shape[1]), F32)], axis=1)
        pre[0, half, 1] = jnp.concatenate([rows, zero8], axis=0).astype(BF)
    text_buf[me_loop] = text[...].astype(F32)

    pl.semaphore_wait(barrier, N_DP - 1 + 2 * (N_LOOP - 1) + 1)

    def whole(ref, sem, recv_sem=None):
        return remote(ref, ref, sem, sem if recv_sem is None else recv_sem, me_loop, sib_dp)

    parity = lax.rem(me_loop // 2, 2)
    mix_of = (0, parity, 1 - parity)

    def slab_of(w, owner_core, where):
        if w == 0:
            return up_buf.at[owner_core, where]
        return mix_buf.at[mix_of[w], where, owner_core]

    def to_sibling(w, where):
        slab = slab_of(w, core, where)
        remote(slab, slab, bulk_send.at[w], bulk_recv.at[w], me_loop, sib_dp).start()

    def to_x(w, where_z, sem):
        slab = slab_of(w, core, where_z * 2 + xlo)
        side = lax.rem(where_z, 2)
        target = me_loop + side * (loop_b - me_loop)
        remote(slab, slab, x_send.at[w], w_recv.at[w, sem], target, xnb_dp).start()

    def to_z(w, where_z, direction, sem):
        slab = slab_of(w, core, where_z * 2 + xlo)
        remote(
            slab, slab, z_send.at[w], w_recv.at[w, sem], me_loop, z_dp(direction * sgn)
        ).start()

    def to_y(where, sem):
        slab = slab_of(1, core, where)
        target = lax.rem(me_loop + 2 * sgn + N_LOOP, N_LOOP)
        remote(slab, slab, y_send, y_recv.at[sem], target, me_dp).start()

    def await_slab(w, where, sem):
        slab = slab_of(w, core, where)
        remote(slab, slab, w_send, w_recv.at[w, sem], me_loop, sib_dp).wait_recv()

    def kind_z(kind):
        offset = -kind if kind <= 4 else kind - 4
        return lax.rem(zed + offset * sgn + N_Z, N_Z)

    def begin(w):
        to_z(w, zed, 1, 0)
        to_z(w, zed, -1, 4)
        to_x(w, zed, 7)
        if w == 1:
            to_y(chip, 0)
        to_sibling(w, chip)

    def z_arrival(w, kind):
        sem = kind - 1
        where_z = kind_z(kind)
        await_slab(w, where_z * 2 + xlo, sem)
        if kind in (1, 2, 3):
            to_z(w, where_z, 1, sem + 1)
        if kind in (5, 6):
            to_z(w, where_z, -1, sem + 1)
        to_x(w, where_z, 7 + kind)
        if w == 1:
            to_y(where_z * 2 + xlo, kind)
        to_sibling(w, where_z * 2 + xlo)

    def x_arrival(w, kind):
        where = kind_z(kind) * 2 + 1 - xlo
        await_slab(w, where, 7 + kind)
        if w == 1:
            to_y(where, 8 + kind)
        to_sibling(w, where)

    def y_arrival(index):
        side = xlo if index < 8 else 1 - xlo
        where = kind_z(index % 8) * 2 + side
        slab = slab_of(2, core, where)
        remote(slab, slab, y_send, y_recv.at[index], me_loop, sib_dp).wait_recv()
        to_sibling(2, where)

    def kinds_at(step):
        z_kinds = [step] if step <= 4 else []
        z_kinds += [4 + step] if step <= 3 else []
        x_kinds = {1: [0], 5: [4]}.get(step, [step - 1, 3 + step])
        return z_kinds, x_kinds

    def turn(w, step):
        if w == 2 and step == 0:
            y_arrival(0)
            return
        z_kinds, x_kinds = kinds_at(step)
        for kind in z_kinds:
            if w == 2:
                y_arrival(kind)
            else:
                z_arrival(w, kind)
        for kind in x_kinds:
            if w == 2:
                y_arrival(8 + kind)
            else:
                x_arrival(w, kind)

    def sixteen(w):
        return up_buf.at[0] if w == 0 else mix_buf.at[0, :, 0]

    def finish(w):
        whole(sixteen(w), bulk_send.at[w], bulk_recv.at[w]).wait_recv()

    pre_copy = remote(
        pre.at[0, 1 - core], pre.at[1, 0], pre_sem.at[0], pre_sem.at[1], me_loop, sib_dp
    )
    pre_copy.start()

    def text_copy(o):
        return remote(
            text_buf.at[me_loop],
            text_buf.at[me_loop],
            text_sem.at[0],
            text_sem.at[1],
            lax.rem(me_loop + o, N_LOOP),
            me_dp,
        )

    def merge(index):
        mine = pre[0, core, index].astype(F32)[:24]
        theirs = pre[1, 0, index].astype(F32)[:24]
        first = core == 0
        joined = jnp.concatenate(
            [jnp.where(first, mine, theirs), jnp.where(first, theirs, mine)], axis=0
        )
        return joined.astype(BF)

    pre_copy.wait_recv()
    up_buf[core, chip] = merge(0)
    begin(0)
    own_mix = jnp.where(parity == 0, w_down[...].astype(F32), merge(1).astype(F32))
    mix_buf[parity, chip, core] = own_mix.astype(BF)

    begin(1)

    width_at = lax.broadcasted_iota(jnp.int32, (16, 128), 0)

    def chunk_lanes(cb):
        return pl.ds(pl.multiple_of(cb * 128, 128), 128)

    def conv_chunk(chunk, carry):
        image, cb = chunk // 6, lax.rem(chunk, 6)
        lanes = chunk_lanes(cb)
        for a in range(7):
            for b in range(7):
                taps[a * 7 + b] = jnp.broadcast_to(kern[a, pl.ds(b, 1), lanes], (8, 128))

        def row(r, state):
            accs, total = state
            x = images[image, r, :, lanes].astype(F32)
            views = []
            for b in range(7):
                if b == 3:
                    view = x
                else:
                    view = pltpu.roll(x, (3 - b) % 16, 0)
                    inside = width_at >= 3 - b if b < 3 else width_at < 19 - b
                    view = jnp.where(inside, view, 0.0)
                shifted[chunk, b, r] = view
                views.append(view.reshape(2, 8, 128))
            fresh = []
            for j in range(7):
                acc = accs[j]
                for b in range(7):
                    acc = acc + views[b] * taps[(6 - j) * 7 + b]
                fresh.append(acc)
            conv_pad[image, r, :, lanes] = fresh[0].reshape(16, 128)
            return (tuple(fresh[1:]) + (jnp.zeros((2, 8, 128), F32),), total + views[3])

        zero = jnp.zeros((2, 8, 128), F32)
        accs, total = lax.fori_loop(0, 16, row, ((zero,) * 7, zero))
        for j in range(3):
            conv_pad[image, 16 + j, :, lanes] = accs[j].reshape(16, 128)
        img_sum[image, :, lanes] = total[0] + total[1]
        return carry

    plan = (
        ((0, 1), (1, 1)),
        ((0, 2), (1, 2), (2, 0)),
        ((0, 3), (1, 3), (2, 1)),
        ((0, 4), (1, 4), (2, 2)),
        ((0, 5), (1, 5), (2, 3)),
        ((2, 4),),
    )
    for group in range(6):
        lax.fori_loop(2 * group, 2 * group + 2, conv_chunk, 0)
        for w, step in plan[group]:
            turn(w, step)

    @pl.loop(1, N_LOOP)
    def _(o):
        text_copy(o).start()

    gain_row = gain[...].reshape(1, C)

    def norm_rows(index, carry):
        image, r = index // 16, lax.rem(index, 16)
        rows = pl.ds(pl.multiple_of(index * 16, 16), 16)
        value = conv_pad[image, r + 3]
        centered = value - jnp.mean(value, axis=-1, keepdims=True)
        inv = lax.rsqrt(jnp.mean(centered * centered, axis=-1, keepdims=True) + EPS)
        hat = centered * inv
        xhat[rows, :] = hat
        rstd[rows, :] = jnp.broadcast_to(inv, (16, 128))
        normed[rows, :] = (hat * gain_row).astype(BF)
        return carry

    lax.fori_loop(0, 32, norm_rows, 0)
    finish(0)

    scale_row = scale[...].reshape(1, C)
    c0 = 0.7978845608028654
    row_at = lax.broadcasted_iota(jnp.int32, (16, C), 0)
    means = []
    for half in range(2):
        hid[...] = jnp.dot(
            normed[...], up_buf[half].reshape(C, C), preferred_element_type=F32
        )
        if half == 0:
            turn(2, 5)
        bias = b_up[half * C : (half + 1) * C].reshape(1, C)
        image_sums = []
        for image in range(2):

            def gelu_rows(index, total):
                rows = pl.ds(pl.multiple_of(image * 256 + index * 16, 16), 16)
                h = hid[rows, :] + bias
                square = h * h
                t = jnp.tanh(c0 * h * (1.0 + 0.044715 * square))
                plus = 0.5 + 0.5 * t
                active = (h * plus).astype(BF).astype(F32)
                gprime[half, rows, :] = plus + (0.5 * c0) * h * (1.0 - t * t) * (
                    1.0 + (3 * 0.044715) * square
                )
                return total + active[:8] + active[8:]

            total = lax.fori_loop(0, 16, gelu_rows, jnp.zeros((8, C), F32))
            image_sums.append(jnp.sum(total, axis=0, keepdims=True) * (1.0 / 256))
        means.append(
            jnp.where(row_at == 0, image_sums[0], jnp.where(row_at == 1, image_sums[1], 0.0))
        )

    finish(1)
    finish(2)
    mlp = jnp.zeros((16, C), F32)
    for half in range(2):
        high = means[half].astype(BF)
        low = (means[half] - high.astype(F32)).astype(BF)
        rows = mix_buf[0, 8 * half : 8 * half + 8].reshape(C, C)
        mlp = mlp + jnp.dot(high, rows, preferred_element_type=F32)
        mlp = mlp + jnp.dot(low, rows, preferred_element_type=F32)
    img_mean = [jnp.sum(img_sum[image], axis=0, keepdims=True) * (1.0 / 256) for image in range(2)]
    img_mean = jnp.where(row_at == 0, img_mean[0], jnp.where(row_at == 1, img_mean[1], 0.0))
    pooled = (img_mean + scale_row * mlp).astype(BF)
    raw = [
        jnp.dot(
            pooled, mix_buf[1, :, half, :, :EH].reshape(C, EH), preferred_element_type=F32
        )
        for half in range(2)
    ]
    norm = lax.rsqrt(
        jnp.sum(raw[0] * raw[0], axis=-1, keepdims=True)
        + jnp.sum(raw[1] * raw[1], axis=-1, keepdims=True)
        + EPS
    )
    emb = jnp.concatenate([raw[0] * norm, raw[1][:, : E - EH] * norm], axis=1)

    whole(text_buf.at[pl.ds(0, N_LOOP - 1)], text_sem.at[0], text_sem.at[1]).wait_recv()
    for l in range(N_LOOP):
        text_all[2 * l : 2 * l + 2, :] = text_buf[l]
    raw_rows = text_all[...]
    text_norm = jnp.sqrt(jnp.sum(raw_rows * raw_rows, axis=-1, keepdims=True) + EPS)
    text_emb = (raw_rows / text_norm).astype(BF).astype(F32)
    logit_scale = jnp.exp(jnp.full((1, 1), log_temp[0], F32))
    logits = logit_scale * nt(emb, text_emb, HI) + loss_bias[0]
    pair_row_at = lax.broadcasted_iota(jnp.int32, (16, GROUP), 0)
    pair_col_at = lax.broadcasted_iota(jnp.int32, (16, GROUP), 1)
    own = jnp.where(pair_row_at == 0, pair[0, 0], pair[0, 1])
    signs = jnp.where(own == pair_col_at, 1.0, -1.0)
    weight = -signs * jax.nn.sigmoid(-signs * logits) / GROUP
    weight = jnp.where(pair_row_at < 2, weight, 0.0)
    image_cot = logit_scale * jnp.dot(weight, text_emb, precision=HI, preferred_element_type=F32)

    msg_buf[me_loop, :, :E] = emb[:2]
    msg_buf[me_loop, :, E:] = jnp.concatenate(
        [weight[:2], jnp.zeros((2, 128 - GROUP), F32)], axis=1
    )

    def msg_copy(o):
        return remote(
            msg_buf.at[me_loop],
            msg_buf.at[me_loop],
            msg_sem.at[0],
            msg_sem.at[1],
            lax.rem(me_loop + o, N_LOOP),
            me_dp,
        )

    d_raw = norm * (image_cot - emb * jnp.sum(image_cot * emb, axis=-1, keepdims=True))
    d_raw = d_raw.astype(BF)
    d_pooled = nt(d_raw[:, :EH], mix_buf[1, :, 0, :, :EH].reshape(C, EH)) + nt(
        d_raw[:, EH:], mix_buf[1, :, 1, :, : E - EH].reshape(C, E - EH)
    )
    d_pooled = d_pooled.astype(BF).astype(F32)
    d_mlp = (scale_row * (d_pooled * (1.0 / 256))).astype(BF)
    for half in range(2):
        value = nt(d_mlp, mix_buf[0, 8 * half : 8 * half + 8].reshape(C, C))
        dact[half] = value.astype(BF).astype(F32)

    def hidden_cot(half):
        for image in range(2):
            factor = dact[half, image : image + 1, :]

            def rows_cot(index, carry):
                rows = pl.ds(pl.multiple_of(image * 256 + index * 16, 16), 16)
                dhid[half, rows, :] = (gprime[half, rows, :] * factor).astype(BF)
                return carry

            lax.fori_loop(0, 16, rows_cot, 0)

    def up_grad_half(half):
        hidden_cot(half)
        g_buf[half] = tn(normed[...], dhid[half]).astype(BF).reshape(16, 48, C)

    up_grad_half(1 - core)
    r1 = remote(g_buf.at[1 - core], rs1, r1_sem.at[0], r1_sem.at[1], me_loop, sib_dp)
    r1.start()
    up_grad_half(core)
    r1.wait_recv()

    def core_sum(where):
        s1[where] = (g_buf[core, where].astype(F32) + rs1[where].astype(F32)).astype(BF)

    def x_copy(z):
        where = z * 2 + 1 - xlo
        target = me_loop + lax.rem(z, 2) * (loop_b - me_loop)
        return remote(s1.at[where], rs2.at[z], r2_send, r2_recv.at[z], target, xnb_dp)

    @pl.loop(1, N_Z + 1)
    def _(o):
        z = lax.rem(zed + o, N_Z)
        core_sum(z * 2 + 1 - xlo)
        x_copy(z).start()

    @pl.loop(0, N_Z)
    def _(z):
        core_sum(z * 2 + xlo)

    @pl.loop(1, N_LOOP)
    def _(o):
        msg_copy(o).start()

    hid[...] = nt(dhid[0], up_buf[0].reshape(C, C)) + nt(dhid[1], up_buf[1].reshape(C, C))

    dconv = conv_pad

    def norm_cot(index, carry):
        rows = pl.ds(pl.multiple_of(index * 16, 16), 16)
        d_hat = hid[rows, :].astype(BF).astype(F32) * gain_row
        hat = xhat[rows, :]
        first = jnp.mean(d_hat, axis=-1, keepdims=True)
        second = jnp.mean(d_hat * hat, axis=-1, keepdims=True)
        dconv[index // 16, lax.rem(index, 16)] = rstd[rows, :1] * (
            d_hat - first - hat * second
        )
        return carry

    lax.fori_loop(0, 32, norm_cot, 0)

    def z_copy(o):
        z = lax.rem(zed + o, N_Z)
        return remote(
            s2.at[z],
            rs3.at[o - 1],
            r3_sem.at[0],
            r3_sem.at[1],
            me_loop,
            z * 4 + xlo * 2 + core,
        )

    def x_sum(z):
        x_copy(z).wait_recv()
        s2[z] = (s1[z * 2 + xlo].astype(F32) + rs2[z].astype(F32)).astype(BF)

    @pl.loop(1, N_Z)
    def _(o):
        x_sum(lax.rem(zed + o, N_Z))
        z_copy(o).start()

    x_sum(zed)

    kg[...] = jnp.zeros(kg.shape, F32)

    summing = (chip < N_SLAB) & (core == lax.rem(chip, 2))

    def slab_copy(slab):
        return remote(
            kg_out.at[slab],
            kr1.at[me_dp],
            p1_sem.at[0],
            p1_sem.at[1],
            me_loop,
            2 * slab + slab % 2,
        )

    tap_at = lax.broadcasted_iota(jnp.int32, (8, 128), 0)

    def kernel_chunk(cb, offset):
        lanes = chunk_lanes(cb)

        def column(b, carry):
            accs = [jnp.zeros((2, 8, 128), F32) for _ in range(7)]
            for image in range(2):
                window = {}
                for r in range(16):
                    view = shifted[image * 6 + cb, b, r].reshape(2, 8, 128)
                    for a in range(7):
                        h = r - a + 3
                        if 0 <= h < 16:
                            if h not in window:
                                value = dconv[image, h, :, lanes]
                                window[h] = value.reshape(2, 8, 128)
                            accs[a] = accs[a] + view * window[h]
            pair = cb // 2
            for a in range(7):
                value = jnp.sum(accs[a][0] + accs[a][1], axis=0, keepdims=True)
                columns = slice(offset, offset + 128)
                kg[pair, a, :, columns] = kg[pair, a, :, columns] + jnp.where(
                    tap_at == b, value, 0.0
                )
            return carry

        lax.fori_loop(0, 7, column, 0)

    for group in range(3):
        kernel_chunk(2 * group, 0)
        kernel_chunk(2 * group + 1, 128)
        for part in range(4):
            slab = group * 4 + part
            kg_out[slab] = kg[group, 2 * part : 2 * part + 2].reshape(16, 256).astype(BF)

            @pl.when(jnp.logical_not(summing) | (chip != slab))
            def _():
                slab_copy(slab).start()

    def share_copy(o):
        return remote(
            kr2.at[me_loop],
            kr2.at[me_loop],
            p2_sem.at[0],
            p2_sem.at[1],
            lax.rem(me_loop + o, N_LOOP),
            me_dp,
        )

    def spread_copy(o):
        return remote(
            k1, kfin.at[chip], p3_sem.at[0], p3_sem.at[1], me_loop, lax.rem(me_dp + o, N_DP)
        )

    def sum_dp(first, last):
        @pl.when(summing & (chip >= first) & (chip < last))
        def _():
            whole(kr1.at[pl.ds(0, N_DP - 1)], p1_sem.at[0], p1_sem.at[1]).wait_recv()
            kr1[me_dp] = kg_out[chip]
            summed = kr1[0].astype(F32)
            for d in range(1, N_DP):
                summed = summed + kr1[d].astype(F32)
            kr2[me_loop] = summed.astype(BF)

            @pl.loop(1, N_LOOP)
            def _(o):
                share_copy(o).start()

    def sum_loop(first, last):
        @pl.when(summing & (chip >= first) & (chip < last))
        def _():
            whole(kr2.at[pl.ds(0, N_LOOP - 1)], p2_sem.at[0], p2_sem.at[1]).wait_recv()
            summed = kr2[0].astype(F32)
            for l in range(1, N_LOOP):
                summed = summed + kr2[l].astype(F32)
            k1[...] = summed.astype(BF)

            @pl.loop(1, N_DP)
            def _(o):
                spread_copy(o).start()

            kfin[chip] = summed.astype(BF)

    sum_dp(0, 8)

    pre_copy.wait_send()
    for w in range(3):
        whole(sixteen(w), bulk_send.at[w]).wait_send()
    for w in range(2):
        whole(up_buf.at[0, pl.ds(0, 7)], z_send.at[w]).wait_send()
        whole(up_buf.at[0, pl.ds(0, 8)], x_send.at[w]).wait_send()
    whole(sixteen(0), y_send).wait_send()
    whole(text_buf.at[pl.ds(0, N_LOOP - 1)], text_sem.at[0]).wait_send()

    whole(msg_buf.at[pl.ds(0, N_LOOP - 1)], msg_sem.at[0], msg_sem.at[1]).wait_recv()
    for l in range(N_LOOP):
        msg_all[2 * l : 2 * l + 2, :] = msg_buf[l]
    all_emb = msg_all[:, :E]
    all_weight = msg_all[:, E:]
    pick_row = lax.broadcasted_iota(jnp.int32, (8, 128), 0)
    pick_col = lax.broadcasted_iota(jnp.int32, (8, 128), 1)
    pick = jnp.where((pick_col == 2 * me_loop + pick_row) & (pick_row < 2), 1.0, 0.0)
    mine = nt(pick, all_weight, HI)
    text_cot = logit_scale * jnp.dot(mine, all_emb, precision=HI, preferred_element_type=F32)
    text_cot = text_cot[:2]
    own_rows = text[...].astype(F32)
    own_norm = jnp.sqrt(jnp.sum(own_rows * own_rows, axis=-1, keepdims=True) + EPS)
    own_hat = own_rows / own_norm
    text_out[...] = (
        text_cot - own_hat * jnp.sum(own_hat * text_cot, axis=-1, keepdims=True)
    ) / own_norm

    total = s2[zed].astype(F32)
    whole(rs3, r3_sem.at[0], r3_sem.at[1]).wait_recv()
    for o in range(1, N_Z):
        total = total + rs3[o - 1].astype(F32)
    for q in range(N_PIECE):
        rb, lh = q // 2, q % 2
        p3[q] = total[rb * 8 : rb * 8 + 8, lh * 384 : lh * 384 + 384]

    def piece_copy(q):
        return remote(p3.at[q], rs4.at[me_loop], r4_sem.at[0], r4_sem.at[1], q, me_dp)

    for q in range(N_PIECE):

        @pl.when(me_loop != q)
        def _():
            piece_copy(q).start()

    sum_dp(8, N_SLAB)
    sum_loop(0, 8)

    target_core = me_loop // 6
    target_dp = chip * 2 + target_core
    own_piece = lax.rem(me_loop, 6)

    def result_copy(o):
        return remote(
            r4,
            fin.at[core * 6 + own_piece],
            r5_sem.at[0],
            r5_sem.at[1],
            lax.rem(me_loop + o, N_LOOP),
            target_dp,
        )

    @pl.when(me_loop < N_PIECE)
    def _():
        whole(rs4.at[pl.ds(0, N_LOOP - 1)], r4_sem.at[0], r4_sem.at[1]).wait_recv()
        rs4[me_loop] = p3[me_loop]
        summed = rs4[0]
        for l in range(1, N_LOOP):
            summed = summed + rs4[l]
        r4[...] = summed

        @pl.loop(1, N_LOOP)
        def _(o):
            result_copy(o).start()

        @pl.when(target_core != core)
        def _():
            remote(
                r4,
                fin.at[core * 6 + own_piece],
                r5_sem.at[0],
                r5_sem.at[1],
                me_loop,
                sib_dp,
            ).start()

        @pl.when(target_core == core)
        def _():
            fin[core * 6 + own_piece] = r4[...]

    sum_loop(8, N_SLAB)

    own_result = (target_core == core) & (me_loop < N_PIECE)

    @pl.when(own_result)
    def _():
        whole(fin.at[pl.ds(0, N_PIECE - 1)], r5_sem.at[0], r5_sem.at[1]).wait_recv()

    @pl.when(jnp.logical_not(own_result))
    def _():
        whole(fin, r5_sem.at[0], r5_sem.at[1]).wait_recv()

    for cs in range(2):
        for j in range(6):
            rb, lh = j // 2, j % 2
            columns = slice(cs * C + lh * 384, cs * C + lh * 384 + 384)
            up_out[rb * 8 : rb * 8 + 8, columns] = fin[cs * 6 + j]

    @pl.when(summing)
    def _():
        some = pl.ds(0, N_SLAB - 1)
        whole(kfin.at[some], p3_sem.at[0], p3_sem.at[1]).wait_recv()
        whole(kg_out.at[some], p1_sem.at[0]).wait_send()
        whole(kr2.at[pl.ds(0, N_LOOP - 1)], p2_sem.at[0]).wait_send()
        whole(kr1.at[pl.ds(0, N_DP - 1)], p3_sem.at[0]).wait_send()

    @pl.when(jnp.logical_not(summing))
    def _():
        whole(kfin, p3_sem.at[0], p3_sem.at[1]).wait_recv()
        whole(kg_out, p1_sem.at[0]).wait_send()

    for slab in range(N_SLAB):
        lp, part = slab // 4, slab % 4
        value = kfin[slab].astype(F32)
        kernel_out[2 * part, :, lp * 256 : lp * 256 + 256] = value[:7]
        if part < 3:
            kernel_out[2 * part + 1, :, lp * 256 : lp * 256 + 256] = value[8:15]

    whole(msg_buf.at[pl.ds(0, N_LOOP - 1)], msg_sem.at[0]).wait_send()
    r1.wait_send()
    whole(rs2, r2_send).wait_send()
    whole(rs3, r3_sem.at[0]).wait_send()

    @pl.when(me_loop < N_PIECE)
    def _():
        whole(p3.at[pl.ds(0, N_PIECE - 1)], r4_sem.at[0]).wait_send()

        @pl.when(target_core != core)
        def _():
            whole(rs4, r5_sem.at[0]).wait_send()

        @pl.when(target_core == core)
        def _():
            whole(rs4.at[pl.ds(0, N_LOOP - 1)], r5_sem.at[0]).wait_send()

    @pl.when(me_loop >= N_PIECE)
    def _():
        whole(p3, r4_sem.at[0]).wait_send()


def body(
    images,
    kernel,
    ln_gain,
    w_up,
    b_up,
    w_down,
    layer_scale,
    w_head,
    text_rows,
    pair_ids,
    log_temp,
    loss_bias,
):
    vmem = pl.BlockSpec(memory_space=pltpu.VMEM)
    smem = pl.BlockSpec(memory_space=pltpu.SMEM)
    dma = pltpu.SemaphoreType.DMA
    scratch = [
        pltpu.VMEM((2, 2, 2, 32, C), BF),
        pltpu.VMEM((2, 16, 48, C), BF),
        pltpu.VMEM((2, 16, 2, 48, C), BF),
        pltpu.VMEM((N_LOOP, 2, E), F32),
        pltpu.VMEM((GROUP, E), F32),
        pltpu.VMEM((49, 8, 128), F32),
        pltpu.VMEM((12, 7, 16, 16, 128), F32),
        pltpu.VMEM((2, 19, 16, C), F32),
        pltpu.VMEM((2, 8, C), F32),
        pltpu.VMEM((512, C), BF),
        pltpu.VMEM((512, C), F32),
        pltpu.VMEM((512, 128), F32),
        pltpu.VMEM((512, C), F32),
        pltpu.VMEM((2, 512, C), F32),
        pltpu.VMEM((2, 16, C), F32),
        pltpu.VMEM((2, 512, C), BF),
        pltpu.VMEM((2, 16, 48, C), BF),
        pltpu.VMEM((16, 48, C), BF),
        pltpu.VMEM((16, 48, C), BF),
        pltpu.VMEM((8, 48, C), BF),
        pltpu.VMEM((8, 48, C), BF),
        pltpu.VMEM((7, 48, C), BF),
        pltpu.VMEM((N_PIECE, 8, 384), F32),
        pltpu.VMEM((N_LOOP, 8, 384), F32),
        pltpu.VMEM((8, 384), F32),
        pltpu.VMEM((N_PIECE, 8, 384), F32),
        pltpu.VMEM((N_LOOP, 2, E + 128), F32),
        pltpu.VMEM((GROUP, E + 128), F32),
        pltpu.VMEM((3, 8, 8, 256), F32),
        pltpu.VMEM((N_SLAB, 16, 256), BF),
        pltpu.VMEM((N_DP, 16, 256), BF),
        pltpu.VMEM((16, 256), BF),
        pltpu.VMEM((N_LOOP, 16, 256), BF),
        pltpu.VMEM((N_SLAB, 16, 256), BF),
        dma,
        dma((2, 15)),
        dma((3,)),
        dma((3,)),
        dma((2,)),
        dma((2,)),
        dma,
        dma((16,)),
        dma((2,)),
        dma((2,)),
        dma((2,)),
        dma((2,)),
        dma,
        dma((N_Z,)),
        dma((2,)),
        dma((2,)),
        dma((2,)),
        dma((2,)),
        dma((2,)),
        dma((2,)),
    ]
    kernel_grad, up_grad, text_grad = pl.pallas_call(
        kernel_body,
        out_shape=(
            jax.ShapeDtypeStruct((7, 7, C), F32),
            jax.ShapeDtypeStruct((24, FFW), F32),
            jax.ShapeDtypeStruct((2, E), F32),
        ),
        in_specs=[vmem] * 9 + [smem] * 3,
        out_specs=(vmem, vmem, vmem),
        scratch_shapes=scratch,
        compiler_params=pltpu.CompilerParams(
            collective_id=0, has_side_effects=True, vmem_limit_bytes=56 * 1024 * 1024
        ),
        name="tower_step",
    )(
        images[0],
        kernel,
        ln_gain,
        w_up,
        b_up,
        w_down,
        layer_scale,
        w_head,
        text_rows[0],
        pair_ids,
        log_temp,
        loss_bias,
    )
    return (kernel_grad, up_grad, text_grad[None])


def solution(mesh):
    placed = (
        P("dp", "loop", None, None, None),
        P(),
        P(),
        P("dp", None),
        P(),
        P("dp", None),
        P(),
        P("dp", None),
        P("dp", "loop", None),
        P("dp", "loop"),
        P(),
        P(),
    )
    return jax.shard_map(
        body,
        mesh=mesh,
        in_specs=placed,
        out_specs=(P(), P("dp", None), P("dp", "loop", None)),
        check_vma=False,
    )
```

```python
import functools

import jax
import jax.numpy as jnp
from jax import lax
from jax.experimental import pallas as pl
from jax.experimental.pallas import tpu as pltpu
from jax.sharding import PartitionSpec as P

MESH = pl.DeviceIdType.MESH
EPS = 1e-06
BF = jnp.bfloat16
F32 = jnp.float32
HI = lax.Precision.HIGHEST

N_LOOP = 16
N_DP = 32
N_Z = 8
C = 768
FFW = 1536
E = 1152
EH = 640
GROUP = 32
N_PIECE = 12
N_SLAB = 12


def nt(a, b, precision=None):
    return lax.dot_general(
        a, b, (((1,), (1,)), ((), ())), preferred_element_type=F32, precision=precision
    )


def tn(a, b):
    return lax.dot_general(a, b, (((0,), (0,)), ((), ())), preferred_element_type=F32)


def kernel_body(
    images,
    kern,
    gain,
    w_up,
    b_up,
    w_down,
    scale,
    w_head,
    text,
    pair,
    log_temp,
    loss_bias,
    kernel_out,
    up_out,
    text_out,
    pre,
    up_buf,
    mix_buf,
    text_buf,
    text_all,
    taps,
    shifted,
    conv_pad,
    img_sum,
    normed,
    xhat,
    rstd,
    hid,
    gprime,
    dact,
    dhid,
    g_buf,
    rs1,
    s1,
    rs2,
    s2,
    rs3,
    p3,
    rs4,
    r4,
    fin,
    msg_buf,
    msg_all,
    kg,
    kg_out,
    kr1,
    k1,
    kr2,
    kfin,
    w_send,
    w_recv,
    bulk_send,
    bulk_recv,
    z_send,
    x_send,
    y_send,
    y_recv,
    pre_sem,
    text_sem,
    msg_sem,
    r1_sem,
    r2_send,
    r2_recv,
    r3_sem,
    r4_sem,
    r5_sem,
    p1_sem,
    p2_sem,
    p3_sem,
):
    me_loop = lax.axis_index("loop")
    me_dp = lax.axis_index("dp")
    core = lax.rem(me_dp, 2)
    xlo = lax.rem(me_dp // 2, 2)
    zed = me_dp // 4
    chip = me_dp // 2
    xhi = lax.rem(me_loop, 2)
    sib_dp = me_dp + 1 - 2 * core
    xnb_dp = me_dp + 2 - 4 * xlo
    loop_b = me_loop + 1 - 2 * xhi
    sgn = 1 - 2 * core

    def z_dp(offset):
        return lax.rem(zed + offset + N_Z, N_Z) * 4 + xlo * 2 + core

    def remote(src, dst, send, recv, loop, dp):
        return pltpu.make_async_remote_copy(
            src_ref=src,
            dst_ref=dst,
            send_sem=send,
            recv_sem=recv,
            device_id=(loop, dp),
            device_id_type=MESH,
        )

    barrier = pltpu.get_barrier_semaphore()

    @pl.loop(1, N_DP)
    def _(o):
        pl.semaphore_signal(
            barrier, inc=1, device_id=(me_loop, lax.rem(me_dp + o, N_DP)), device_id_type=MESH
        )

    @pl.loop(1, N_LOOP)
    def _(o):
        other = lax.rem(me_loop + o, N_LOOP)
        pl.semaphore_signal(barrier, inc=1, device_id=(other, me_dp), device_id_type=MESH)
        pl.semaphore_signal(barrier, inc=1, device_id=(other, sib_dp), device_id_type=MESH)

    pl.semaphore_signal(barrier, inc=1, device_id=(loop_b, xnb_dp), device_id_type=MESH)

    zero8 = jnp.zeros((8, C), F32)
    for half in range(2):
        rows = w_up[:, half * C : (half + 1) * C].astype(F32)
        pre[0, half, 0] = jnp.concatenate([rows, zero8], axis=0).astype(BF)
        rows = w_head[:, half * EH : min((half + 1) * EH, E)].astype(F32)
        rows = jnp.concatenate([rows, jnp.zeros((24, C - rows.shape[1]), F32)], axis=1)
        pre[0, half, 1] = jnp.concatenate([rows, zero8], axis=0).astype(BF)
    text_buf[me_loop] = text[...].astype(F32)

    pl.semaphore_wait(barrier, N_DP - 1 + 2 * (N_LOOP - 1) + 1)

    def whole(ref, sem, recv_sem=None):
        return remote(ref, ref, sem, sem if recv_sem is None else recv_sem, me_loop, sib_dp)

    parity = lax.rem(me_loop // 2, 2)
    mix_of = (0, parity, 1 - parity)

    def slab_of(w, owner_core, where):
        if w == 0:
            return up_buf.at[owner_core, where]
        return mix_buf.at[mix_of[w], where, owner_core]

    def to_sibling(w, where):
        slab = slab_of(w, core, where)
        remote(slab, slab, bulk_send.at[w], bulk_recv.at[w], me_loop, sib_dp).start()

    def to_x(w, where_z, sem):
        slab = slab_of(w, core, where_z * 2 + xlo)
        side = lax.rem(where_z, 2)
        target = me_loop + side * (loop_b - me_loop)
        remote(slab, slab, x_send.at[w], w_recv.at[w, sem], target, xnb_dp).start()

    def to_z(w, where_z, direction, sem):
        slab = slab_of(w, core, where_z * 2 + xlo)
        remote(
            slab, slab, z_send.at[w], w_recv.at[w, sem], me_loop, z_dp(direction * sgn)
        ).start()

    def to_y(where, sem):
        slab = slab_of(1, core, where)
        target = lax.rem(me_loop + 2 * sgn + N_LOOP, N_LOOP)
        remote(slab, slab, y_send, y_recv.at[sem], target, me_dp).start()

    def await_slab(w, where, sem):
        slab = slab_of(w, core, where)
        remote(slab, slab, w_send, w_recv.at[w, sem], me_loop, sib_dp).wait_recv()

    def kind_z(kind):
        offset = -kind if kind <= 4 else kind - 4
        return lax.rem(zed + offset * sgn + N_Z, N_Z)

    def begin(w):
        to_z(w, zed, 1, 0)
        to_z(w, zed, -1, 4)
        to_x(w, zed, 7)
        if w == 1:
            to_y(chip, 0)
        to_sibling(w, chip)

    def z_arrival(w, kind):
        sem = kind - 1
        where_z = kind_z(kind)
        await_slab(w, where_z * 2 + xlo, sem)
        if kind in (1, 2, 3):
            to_z(w, where_z, 1, sem + 1)
        if kind in (5, 6):
            to_z(w, where_z, -1, sem + 1)
        to_x(w, where_z, 7 + kind)
        if w == 1:
            to_y(where_z * 2 + xlo, kind)
        to_sibling(w, where_z * 2 + xlo)

    def x_arrival(w, kind):
        where = kind_z(kind) * 2 + 1 - xlo
        await_slab(w, where, 7 + kind)
        if w == 1:
            to_y(where, 8 + kind)
        to_sibling(w, where)

    def y_arrival(index):
        side = xlo if index < 8 else 1 - xlo
        where = kind_z(index % 8) * 2 + side
        slab = slab_of(2, core, where)
        remote(slab, slab, y_send, y_recv.at[index], me_loop, sib_dp).wait_recv()
        to_sibling(2, where)

    def kinds_at(step):
        z_kinds = [step] if step <= 4 else []
        z_kinds += [4 + step] if step <= 3 else []
        x_kinds = {1: [0], 5: [4]}.get(step, [step - 1, 3 + step])
        return z_kinds, x_kinds

    def turn(w, step):
        if w == 2 and step == 0:
            y_arrival(0)
            return
        z_kinds, x_kinds = kinds_at(step)
        for kind in z_kinds:
            if w == 2:
                y_arrival(kind)
            else:
                z_arrival(w, kind)
        for kind in x_kinds:
            if w == 2:
                y_arrival(8 + kind)
            else:
                x_arrival(w, kind)

    def sixteen(w):
        return up_buf.at[0] if w == 0 else mix_buf.at[0, :, 0]

    def finish(w):
        whole(sixteen(w), bulk_send.at[w], bulk_recv.at[w]).wait_recv()

    pre_copy = remote(
        pre.at[0, 1 - core], pre.at[1, 0], pre_sem.at[0], pre_sem.at[1], me_loop, sib_dp
    )
    pre_copy.start()

    def text_copy(o):
        return remote(
            text_buf.at[me_loop],
            text_buf.at[me_loop],
            text_sem.at[0],
            text_sem.at[1],
            lax.rem(me_loop + o, N_LOOP),
            me_dp,
        )

    def merge(index):
        mine = pre[0, core, index].astype(F32)[:24]
        theirs = pre[1, 0, index].astype(F32)[:24]
        first = core == 0
        joined = jnp.concatenate(
            [jnp.where(first, mine, theirs), jnp.where(first, theirs, mine)], axis=0
        )
        return joined.astype(BF)

    pre_copy.wait_recv()
    up_buf[core, chip] = merge(0)
    begin(0)
    own_mix = jnp.where(parity == 0, w_down[...].astype(F32), merge(1).astype(F32))
    mix_buf[parity, chip, core] = own_mix.astype(BF)

    begin(1)

    width_at = lax.broadcasted_iota(jnp.int32, (16, 128), 0)

    def chunk_lanes(cb):
        return pl.ds(pl.multiple_of(cb * 128, 128), 128)

    def conv_chunk(chunk, carry):
        image, cb = chunk // 6, lax.rem(chunk, 6)
        lanes = chunk_lanes(cb)
        for a in range(7):
            for b in range(7):
                taps[a * 7 + b] = jnp.broadcast_to(kern[a, pl.ds(b, 1), lanes], (8, 128))

        def row(r, state):
            accs, total = state
            x = images[image, r, :, lanes].astype(F32)
            views = []
            for b in range(7):
                if b == 3:
                    view = x
                else:
                    view = pltpu.roll(x, (3 - b) % 16, 0)
                    inside = width_at >= 3 - b if b < 3 else width_at < 19 - b
                    view = jnp.where(inside, view, 0.0)
                shifted[chunk, b, r] = view
                views.append(view.reshape(2, 8, 128))
            fresh = []
            for j in range(7):
                acc = accs[j]
                for b in range(7):
                    acc = acc + views[b] * taps[(6 - j) * 7 + b]
                fresh.append(acc)
            conv_pad[image, r, :, lanes] = fresh[0].reshape(16, 128)
            return (tuple(fresh[1:]) + (jnp.zeros((2, 8, 128), F32),), total + views[3])

        zero = jnp.zeros((2, 8, 128), F32)
        accs, total = lax.fori_loop(0, 16, row, ((zero,) * 7, zero))
        for j in range(3):
            conv_pad[image, 16 + j, :, lanes] = accs[j].reshape(16, 128)
        img_sum[image, :, lanes] = total[0] + total[1]
        return carry

    plan = (
        ((0, 1), (1, 1)),
        ((0, 2), (1, 2), (2, 0)),
        ((0, 3), (1, 3), (2, 1)),
        ((0, 4), (1, 4), (2, 2)),
        ((0, 5), (1, 5), (2, 3)),
        ((2, 4),),
    )
    for group in range(6):
        lax.fori_loop(2 * group, 2 * group + 2, conv_chunk, 0)
        for w, step in plan[group]:
            turn(w, step)

    @pl.loop(1, N_LOOP)
    def _(o):
        text_copy(o).start()

    gain_row = gain[...].reshape(1, C)

    def norm_rows(index, carry):
        image, r = index // 16, lax.rem(index, 16)
        rows = pl.ds(pl.multiple_of(index * 16, 16), 16)
        value = conv_pad[image, r + 3]
        centered = value - jnp.mean(value, axis=-1, keepdims=True)
        inv = lax.rsqrt(jnp.mean(centered * centered, axis=-1, keepdims=True) + EPS)
        hat = centered * inv
        xhat[rows, :] = hat
        rstd[rows, :] = jnp.broadcast_to(inv, (16, 128))
        normed[rows, :] = (hat * gain_row).astype(BF)
        return carry

    lax.fori_loop(0, 32, norm_rows, 0)
    finish(0)

    scale_row = scale[...].reshape(1, C)
    c0 = 0.7978845608028654
    row_at = lax.broadcasted_iota(jnp.int32, (16, C), 0)
    means = []
    for half in range(2):
        hid[...] = jnp.dot(
            normed[...], up_buf[half].reshape(C, C), preferred_element_type=F32
        )
        if half == 0:
            turn(2, 5)
        bias = b_up[half * C : (half + 1) * C].reshape(1, C)
        image_sums = []
        for image in range(2):

            def gelu_rows(index, total):
                rows = pl.ds(pl.multiple_of(image * 256 + index * 16, 16), 16)
                h = hid[rows, :] + bias
                square = h * h
                t = jnp.tanh(c0 * h * (1.0 + 0.044715 * square))
                plus = 0.5 + 0.5 * t
                active = (h * plus).astype(BF).astype(F32)
                gprime[half, rows, :] = plus + (0.5 * c0) * h * (1.0 - t * t) * (
                    1.0 + (3 * 0.044715) * square
                )
                return total + active[:8] + active[8:]

            total = lax.fori_loop(0, 16, gelu_rows, jnp.zeros((8, C), F32))
            image_sums.append(jnp.sum(total, axis=0, keepdims=True) * (1.0 / 256))
        means.append(
            jnp.where(row_at == 0, image_sums[0], jnp.where(row_at == 1, image_sums[1], 0.0))
        )

    finish(1)
    finish(2)
    mlp = jnp.zeros((16, C), F32)
    for half in range(2):
        high = means[half].astype(BF)
        low = (means[half] - high.astype(F32)).astype(BF)
        rows = mix_buf[0, 8 * half : 8 * half + 8].reshape(C, C)
        mlp = mlp + jnp.dot(high, rows, preferred_element_type=F32)
        mlp = mlp + jnp.dot(low, rows, preferred_element_type=F32)
    img_mean = [jnp.sum(img_sum[image], axis=0, keepdims=True) * (1.0 / 256) for image in range(2)]
    img_mean = jnp.where(row_at == 0, img_mean[0], jnp.where(row_at == 1, img_mean[1], 0.0))
    pooled = (img_mean + scale_row * mlp).astype(BF)
    raw = [
        jnp.dot(
            pooled, mix_buf[1, :, half, :, :EH].reshape(C, EH), preferred_element_type=F32
        )
        for half in range(2)
    ]
    norm = lax.rsqrt(
        jnp.sum(raw[0] * raw[0], axis=-1, keepdims=True)
        + jnp.sum(raw[1] * raw[1], axis=-1, keepdims=True)
        + EPS
    )
    emb = jnp.concatenate([raw[0] * norm, raw[1][:, : E - EH] * norm], axis=1)

    whole(text_buf.at[pl.ds(0, N_LOOP - 1)], text_sem.at[0], text_sem.at[1]).wait_recv()
    for l in range(N_LOOP):
        text_all[2 * l : 2 * l + 2, :] = text_buf[l]
    raw_rows = text_all[...]
    text_norm = jnp.sqrt(jnp.sum(raw_rows * raw_rows, axis=-1, keepdims=True) + EPS)
    text_emb = (raw_rows / text_norm).astype(BF).astype(F32)
    logit_scale = jnp.exp(jnp.full((1, 1), log_temp[0], F32))
    logits = logit_scale * nt(emb, text_emb, HI) + loss_bias[0]
    pair_row_at = lax.broadcasted_iota(jnp.int32, (16, GROUP), 0)
    pair_col_at = lax.broadcasted_iota(jnp.int32, (16, GROUP), 1)
    own = jnp.where(pair_row_at == 0, pair[0, 0], pair[0, 1])
    signs = jnp.where(own == pair_col_at, 1.0, -1.0)
    weight = -signs * jax.nn.sigmoid(-signs * logits) / GROUP
    weight = jnp.where(pair_row_at < 2, weight, 0.0)
    image_cot = logit_scale * jnp.dot(weight, text_emb, precision=HI, preferred_element_type=F32)

    msg_buf[me_loop, :, :E] = emb[:2]
    msg_buf[me_loop, :, E:] = jnp.concatenate(
        [weight[:2], jnp.zeros((2, 128 - GROUP), F32)], axis=1
    )

    def msg_copy(o):
        return remote(
            msg_buf.at[me_loop],
            msg_buf.at[me_loop],
            msg_sem.at[0],
            msg_sem.at[1],
            lax.rem(me_loop + o, N_LOOP),
            me_dp,
        )

    d_raw = norm * (image_cot - emb * jnp.sum(image_cot * emb, axis=-1, keepdims=True))
    d_raw = d_raw.astype(BF)
    d_pooled = nt(d_raw[:, :EH], mix_buf[1, :, 0, :, :EH].reshape(C, EH)) + nt(
        d_raw[:, EH:], mix_buf[1, :, 1, :, : E - EH].reshape(C, E - EH)
    )
    d_pooled = d_pooled.astype(BF).astype(F32)
    d_mlp = (scale_row * (d_pooled * (1.0 / 256))).astype(BF)
    for half in range(2):
        value = nt(d_mlp, mix_buf[0, 8 * half : 8 * half + 8].reshape(C, C))
        dact[half] = value.astype(BF).astype(F32)

    def hidden_cot(half):
        for image in range(2):
            factor = dact[half, image : image + 1, :]

            def rows_cot(index, carry):
                rows = pl.ds(pl.multiple_of(image * 256 + index * 16, 16), 16)
                dhid[half, rows, :] = (gprime[half, rows, :] * factor).astype(BF)
                return carry

            lax.fori_loop(0, 16, rows_cot, 0)

    def up_grad_half(half):
        hidden_cot(half)
        g_buf[half] = tn(normed[...], dhid[half]).astype(BF).reshape(16, 48, C)

    up_grad_half(1 - core)
    r1 = remote(g_buf.at[1 - core], rs1, r1_sem.at[0], r1_sem.at[1], me_loop, sib_dp)
    r1.start()
    up_grad_half(core)

    @pl.loop(1, N_LOOP)
    def _(o):
        msg_copy(o).start()

    r1.wait_recv()

    def core_sum(where):
        s1[where] = (g_buf[core, where].astype(F32) + rs1[where].astype(F32)).astype(BF)

    def x_copy(z):
        where = z * 2 + 1 - xlo
        target = me_loop + lax.rem(z, 2) * (loop_b - me_loop)
        return remote(s1.at[where], rs2.at[z], r2_send, r2_recv.at[z], target, xnb_dp)

    @pl.loop(1, N_Z + 1)
    def _(o):
        z = lax.rem(zed + o, N_Z)
        core_sum(z * 2 + 1 - xlo)
        x_copy(z).start()

    @pl.loop(0, N_Z)
    def _(z):
        core_sum(z * 2 + xlo)

    hid[...] = nt(dhid[0], up_buf[0].reshape(C, C)) + nt(dhid[1], up_buf[1].reshape(C, C))

    dconv = conv_pad

    def norm_cot(index, carry):
        rows = pl.ds(pl.multiple_of(index * 16, 16), 16)
        d_hat = hid[rows, :].astype(BF).astype(F32) * gain_row
        hat = xhat[rows, :]
        first = jnp.mean(d_hat, axis=-1, keepdims=True)
        second = jnp.mean(d_hat * hat, axis=-1, keepdims=True)
        dconv[index // 16, lax.rem(index, 16)] = rstd[rows, :1] * (
            d_hat - first - hat * second
        )
        return carry

    lax.fori_loop(0, 32, norm_cot, 0)

    def z_copy(o):
        z = lax.rem(zed + o, N_Z)
        return remote(
            s2.at[z],
            rs3.at[o - 1],
            r3_sem.at[0],
            r3_sem.at[1],
            me_loop,
            z * 4 + xlo * 2 + core,
        )

    def x_sum(z):
        x_copy(z).wait_recv()
        s2[z] = (s1[z * 2 + xlo].astype(F32) + rs2[z].astype(F32)).astype(BF)

    @pl.loop(1, 5)
    def _(o):
        x_sum(lax.rem(zed + o, N_Z))
        z_copy(o).start()

    kg[...] = jnp.zeros(kg.shape, F32)

    summing = (chip < N_SLAB) & (core == lax.rem(chip, 2))

    def slab_copy(slab):
        return remote(
            kg_out.at[slab],
            kr1.at[me_dp],
            p1_sem.at[0],
            p1_sem.at[1],
            me_loop,
            2 * slab + slab % 2,
        )

    tap_at = lax.broadcasted_iota(jnp.int32, (8, 128), 0)

    def kernel_chunk(cb, offset):
        lanes = chunk_lanes(cb)

        def column(b, carry):
            accs = [jnp.zeros((2, 8, 128), F32) for _ in range(7)]
            for image in range(2):
                window = {}
                for r in range(16):
                    view = shifted[image * 6 + cb, b, r].reshape(2, 8, 128)
                    for a in range(7):
                        h = r - a + 3
                        if 0 <= h < 16:
                            if h not in window:
                                value = dconv[image, h, :, lanes]
                                window[h] = value.reshape(2, 8, 128)
                            accs[a] = accs[a] + view * window[h]
            pair = cb // 2
            for a in range(7):
                value = jnp.sum(accs[a][0] + accs[a][1], axis=0, keepdims=True)
                columns = slice(offset, offset + 128)
                kg[pair, a, :, columns] = kg[pair, a, :, columns] + jnp.where(
                    tap_at == b, value, 0.0
                )
            return carry

        lax.fori_loop(0, 7, column, 0)

    for group in range(3):
        kernel_chunk(2 * group, 0)
        kernel_chunk(2 * group + 1, 128)
        if group == 0:

            @pl.loop(5, N_Z)
            def _(o):
                x_sum(lax.rem(zed + o, N_Z))
                z_copy(o).start()

            x_sum(zed)

        for part in range(4):
            slab = group * 4 + part
            kg_out[slab] = kg[group, 2 * part : 2 * part + 2].reshape(16, 256).astype(BF)

            @pl.when(jnp.logical_not(summing) | (chip != slab))
            def _():
                slab_copy(slab).start()

    def share_copy(o):
        return remote(
            kr2.at[me_loop],
            kr2.at[me_loop],
            p2_sem.at[0],
            p2_sem.at[1],
            lax.rem(me_loop + o, N_LOOP),
            me_dp,
        )

    def spread_copy(o):
        return remote(
            k1, kfin.at[chip], p3_sem.at[0], p3_sem.at[1], me_loop, lax.rem(me_dp + o, N_DP)
        )

    def sum_dp(first, last):
        @pl.when(summing & (chip >= first) & (chip < last))
        def _():
            whole(kr1.at[pl.ds(0, N_DP - 1)], p1_sem.at[0], p1_sem.at[1]).wait_recv()
            kr1[me_dp] = kg_out[chip]
            summed = kr1[0].astype(F32)
            for d in range(1, N_DP):
                summed = summed + kr1[d].astype(F32)
            kr2[me_loop] = summed.astype(BF)

            @pl.loop(1, N_LOOP)
            def _(o):
                share_copy(o).start()

    def sum_loop(first, last):
        @pl.when(summing & (chip >= first) & (chip < last))
        def _():
            whole(kr2.at[pl.ds(0, N_LOOP - 1)], p2_sem.at[0], p2_sem.at[1]).wait_recv()
            summed = kr2[0].astype(F32)
            for l in range(1, N_LOOP):
                summed = summed + kr2[l].astype(F32)
            k1[...] = summed.astype(BF)

            @pl.loop(1, N_DP)
            def _(o):
                spread_copy(o).start()

            kfin[chip] = summed.astype(BF)

    sum_dp(0, 8)

    pre_copy.wait_send()
    for w in range(3):
        whole(sixteen(w), bulk_send.at[w]).wait_send()
    for w in range(2):
        whole(up_buf.at[0, pl.ds(0, 7)], z_send.at[w]).wait_send()
        whole(up_buf.at[0, pl.ds(0, 8)], x_send.at[w]).wait_send()
    whole(sixteen(0), y_send).wait_send()
    whole(text_buf.at[pl.ds(0, N_LOOP - 1)], text_sem.at[0]).wait_send()

    whole(msg_buf.at[pl.ds(0, N_LOOP - 1)], msg_sem.at[0], msg_sem.at[1]).wait_recv()
    for l in range(N_LOOP):
        msg_all[2 * l : 2 * l + 2, :] = msg_buf[l]
    all_emb = msg_all[:, :E]
    all_weight = msg_all[:, E:]
    pick_row = lax.broadcasted_iota(jnp.int32, (8, 128), 0)
    pick_col = lax.broadcasted_iota(jnp.int32, (8, 128), 1)
    pick = jnp.where((pick_col == 2 * me_loop + pick_row) & (pick_row < 2), 1.0, 0.0)
    mine = nt(pick, all_weight, HI)
    text_cot = logit_scale * jnp.dot(mine, all_emb, precision=HI, preferred_element_type=F32)
    text_cot = text_cot[:2]
    own_rows = text[...].astype(F32)
    own_norm = jnp.sqrt(jnp.sum(own_rows * own_rows, axis=-1, keepdims=True) + EPS)
    own_hat = own_rows / own_norm
    text_out[...] = (
        text_cot - own_hat * jnp.sum(own_hat * text_cot, axis=-1, keepdims=True)
    ) / own_norm

    total = s2[zed].astype(F32)
    whole(rs3, r3_sem.at[0], r3_sem.at[1]).wait_recv()
    for o in range(1, N_Z):
        total = total + rs3[o - 1].astype(F32)
    for q in range(N_PIECE):
        rb, lh = q // 2, q % 2
        p3[q] = total[rb * 8 : rb * 8 + 8, lh * 384 : lh * 384 + 384]

    def piece_copy(q):
        return remote(p3.at[q], rs4.at[me_loop], r4_sem.at[0], r4_sem.at[1], q, me_dp)

    for q in range(N_PIECE):

        @pl.when(me_loop != q)
        def _():
            piece_copy(q).start()

    sum_dp(8, N_SLAB)
    sum_loop(0, 8)

    target_core = me_loop // 6
    target_dp = chip * 2 + target_core
    own_piece = lax.rem(me_loop, 6)

    def result_copy(o):
        return remote(
            r4,
            fin.at[core * 6 + own_piece],
            r5_sem.at[0],
            r5_sem.at[1],
            lax.rem(me_loop + o, N_LOOP),
            target_dp,
        )

    @pl.when(me_loop < N_PIECE)
    def _():
        whole(rs4.at[pl.ds(0, N_LOOP - 1)], r4_sem.at[0], r4_sem.at[1]).wait_recv()
        rs4[me_loop] = p3[me_loop]
        summed = rs4[0]
        for l in range(1, N_LOOP):
            summed = summed + rs4[l]
        r4[...] = summed

        @pl.loop(1, N_LOOP)
        def _(o):
            result_copy(o).start()

        @pl.when(target_core != core)
        def _():
            remote(
                r4,
                fin.at[core * 6 + own_piece],
                r5_sem.at[0],
                r5_sem.at[1],
                me_loop,
                sib_dp,
            ).start()

        @pl.when(target_core == core)
        def _():
            fin[core * 6 + own_piece] = r4[...]

    sum_loop(8, N_SLAB)

    own_result = (target_core == core) & (me_loop < N_PIECE)

    @pl.when(own_result)
    def _():
        whole(fin.at[pl.ds(0, N_PIECE - 1)], r5_sem.at[0], r5_sem.at[1]).wait_recv()

    @pl.when(jnp.logical_not(own_result))
    def _():
        whole(fin, r5_sem.at[0], r5_sem.at[1]).wait_recv()

    for cs in range(2):
        for j in range(6):
            rb, lh = j // 2, j % 2
            columns = slice(cs * C + lh * 384, cs * C + lh * 384 + 384)
            up_out[rb * 8 : rb * 8 + 8, columns] = fin[cs * 6 + j]

    @pl.when(summing)
    def _():
        some = pl.ds(0, N_SLAB - 1)
        whole(kfin.at[some], p3_sem.at[0], p3_sem.at[1]).wait_recv()
        whole(kg_out.at[some], p1_sem.at[0]).wait_send()
        whole(kr2.at[pl.ds(0, N_LOOP - 1)], p2_sem.at[0]).wait_send()
        whole(kr1.at[pl.ds(0, N_DP - 1)], p3_sem.at[0]).wait_send()

    @pl.when(jnp.logical_not(summing))
    def _():
        whole(kfin, p3_sem.at[0], p3_sem.at[1]).wait_recv()
        whole(kg_out, p1_sem.at[0]).wait_send()

    for slab in range(N_SLAB):
        lp, part = slab // 4, slab % 4
        value = kfin[slab].astype(F32)
        kernel_out[2 * part, :, lp * 256 : lp * 256 + 256] = value[:7]
        if part < 3:
            kernel_out[2 * part + 1, :, lp * 256 : lp * 256 + 256] = value[8:15]

    whole(msg_buf.at[pl.ds(0, N_LOOP - 1)], msg_sem.at[0]).wait_send()
    r1.wait_send()
    whole(rs2, r2_send).wait_send()
    whole(rs3, r3_sem.at[0]).wait_send()

    @pl.when(me_loop < N_PIECE)
    def _():
        whole(p3.at[pl.ds(0, N_PIECE - 1)], r4_sem.at[0]).wait_send()

        @pl.when(target_core != core)
        def _():
            whole(rs4, r5_sem.at[0]).wait_send()

        @pl.when(target_core == core)
        def _():
            whole(rs4.at[pl.ds(0, N_LOOP - 1)], r5_sem.at[0]).wait_send()

    @pl.when(me_loop >= N_PIECE)
    def _():
        whole(p3, r4_sem.at[0]).wait_send()


def body(
    images,
    kernel,
    ln_gain,
    w_up,
    b_up,
    w_down,
    layer_scale,
    w_head,
    text_rows,
    pair_ids,
    log_temp,
    loss_bias,
):
    vmem = pl.BlockSpec(memory_space=pltpu.VMEM)
    smem = pl.BlockSpec(memory_space=pltpu.SMEM)
    dma = pltpu.SemaphoreType.DMA
    scratch = [
        pltpu.VMEM((2, 2, 2, 32, C), BF),
        pltpu.VMEM((2, 16, 48, C), BF),
        pltpu.VMEM((2, 16, 2, 48, C), BF),
        pltpu.VMEM((N_LOOP, 2, E), F32),
        pltpu.VMEM((GROUP, E), F32),
        pltpu.VMEM((49, 8, 128), F32),
        pltpu.VMEM((12, 7, 16, 16, 128), F32),
        pltpu.VMEM((2, 19, 16, C), F32),
        pltpu.VMEM((2, 8, C), F32),
        pltpu.VMEM((512, C), BF),
        pltpu.VMEM((512, C), F32),
        pltpu.VMEM((512, 128), F32),
        pltpu.VMEM((512, C), F32),
        pltpu.VMEM((2, 512, C), F32),
        pltpu.VMEM((2, 16, C), F32),
        pltpu.VMEM((2, 512, C), BF),
        pltpu.VMEM((2, 16, 48, C), BF),
        pltpu.VMEM((16, 48, C), BF),
        pltpu.VMEM((16, 48, C), BF),
        pltpu.VMEM((8, 48, C), BF),
        pltpu.VMEM((8, 48, C), BF),
        pltpu.VMEM((7, 48, C), BF),
        pltpu.VMEM((N_PIECE, 8, 384), F32),
        pltpu.VMEM((N_LOOP, 8, 384), F32),
        pltpu.VMEM((8, 384), F32),
        pltpu.VMEM((N_PIECE, 8, 384), F32),
        pltpu.VMEM((N_LOOP, 2, E + 128), F32),
        pltpu.VMEM((GROUP, E + 128), F32),
        pltpu.VMEM((3, 8, 8, 256), F32),
        pltpu.VMEM((N_SLAB, 16, 256), BF),
        pltpu.VMEM((N_DP, 16, 256), BF),
        pltpu.VMEM((16, 256), BF),
        pltpu.VMEM((N_LOOP, 16, 256), BF),
        pltpu.VMEM((N_SLAB, 16, 256), BF),
        dma,
        dma((2, 15)),
        dma((3,)),
        dma((3,)),
        dma((2,)),
        dma((2,)),
        dma,
        dma((16,)),
        dma((2,)),
        dma((2,)),
        dma((2,)),
        dma((2,)),
        dma,
        dma((N_Z,)),
        dma((2,)),
        dma((2,)),
        dma((2,)),
        dma((2,)),
        dma((2,)),
        dma((2,)),
    ]
    kernel_grad, up_grad, text_grad = pl.pallas_call(
        kernel_body,
        out_shape=(
            jax.ShapeDtypeStruct((7, 7, C), F32),
            jax.ShapeDtypeStruct((24, FFW), F32),
            jax.ShapeDtypeStruct((2, E), F32),
        ),
        in_specs=[vmem] * 9 + [smem] * 3,
        out_specs=(vmem, vmem, vmem),
        scratch_shapes=scratch,
        compiler_params=pltpu.CompilerParams(
            collective_id=0, has_side_effects=True, vmem_limit_bytes=56 * 1024 * 1024
        ),
        name="tower_step",
    )(
        images[0],
        kernel,
        ln_gain,
        w_up,
        b_up,
        w_down,
        layer_scale,
        w_head,
        text_rows[0],
        pair_ids,
        log_temp,
        loss_bias,
    )
    return (kernel_grad, up_grad, text_grad[None])


def solution(mesh):
    placed = (
        P("dp", "loop", None, None, None),
        P(),
        P(),
        P("dp", None),
        P(),
        P("dp", None),
        P(),
        P("dp", None),
        P("dp", "loop", None),
        P("dp", "loop"),
        P(),
        P(),
    )
    return jax.shard_map(
        body,
        mesh=mesh,
        in_specs=placed,
        out_specs=(P(), P("dp", None), P("dp", "loop", None)),
        check_vma=False,
    )
```

```python
import functools

import jax
import jax.numpy as jnp
from jax import lax
from jax.experimental import pallas as pl
from jax.experimental.pallas import tpu as pltpu
from jax.sharding import PartitionSpec as P

MESH = pl.DeviceIdType.MESH
EPS = 1e-06
BF = jnp.bfloat16
F32 = jnp.float32
HI = lax.Precision.HIGHEST

N_LOOP = 16
N_DP = 32
N_Z = 8
C = 768
FFW = 1536
E = 1152
EH = 640
GROUP = 32
N_PIECE = 12
N_SLAB = 12


def nt(a, b, precision=None):
    return lax.dot_general(
        a, b, (((1,), (1,)), ((), ())), preferred_element_type=F32, precision=precision
    )


def tn(a, b):
    return lax.dot_general(a, b, (((0,), (0,)), ((), ())), preferred_element_type=F32)


def kernel_body(
    images,
    kern,
    gain,
    w_up,
    b_up,
    w_down,
    scale,
    w_head,
    text,
    pair,
    log_temp,
    loss_bias,
    kernel_out,
    up_out,
    text_out,
    pre,
    up_buf,
    mix_buf,
    text_buf,
    text_all,
    taps,
    shifted,
    conv_pad,
    img_sum,
    normed,
    xhat,
    rstd,
    hid,
    gprime,
    dact,
    dhid,
    g_buf,
    rs1,
    s1,
    rs2,
    s2,
    rs3,
    p3,
    rs4,
    r4,
    fin,
    msg_buf,
    msg_all,
    kg,
    kg_out,
    kr1,
    k1,
    kr2,
    kfin,
    w_send,
    w_recv,
    bulk_send,
    bulk_recv,
    z_send,
    x_send,
    y_send,
    y_recv,
    pre_sem,
    text_sem,
    msg_sem,
    r1_sem,
    r2_send,
    r2_recv,
    r3_sem,
    r4_sem,
    r5_sem,
    p1_sem,
    p2_sem,
    p3_sem,
):
    me_loop = lax.axis_index("loop")
    me_dp = lax.axis_index("dp")
    core = lax.rem(me_dp, 2)
    xlo = lax.rem(me_dp // 2, 2)
    zed = me_dp // 4
    chip = me_dp // 2
    xhi = lax.rem(me_loop, 2)
    sib_dp = me_dp + 1 - 2 * core
    xnb_dp = me_dp + 2 - 4 * xlo
    loop_b = me_loop + 1 - 2 * xhi
    sgn = 1 - 2 * core

    def z_dp(offset):
        return lax.rem(zed + offset + N_Z, N_Z) * 4 + xlo * 2 + core

    def remote(src, dst, send, recv, loop, dp):
        return pltpu.make_async_remote_copy(
            src_ref=src,
            dst_ref=dst,
            send_sem=send,
            recv_sem=recv,
            device_id=(loop, dp),
            device_id_type=MESH,
        )

    barrier = pltpu.get_barrier_semaphore()

    @pl.loop(1, N_DP)
    def _(o):
        pl.semaphore_signal(
            barrier, inc=1, device_id=(me_loop, lax.rem(me_dp + o, N_DP)), device_id_type=MESH
        )

    @pl.loop(1, N_LOOP)
    def _(o):
        other = lax.rem(me_loop + o, N_LOOP)
        pl.semaphore_signal(barrier, inc=1, device_id=(other, me_dp), device_id_type=MESH)
        pl.semaphore_signal(barrier, inc=1, device_id=(other, sib_dp), device_id_type=MESH)

    pl.semaphore_signal(barrier, inc=1, device_id=(loop_b, xnb_dp), device_id_type=MESH)

    zero8 = jnp.zeros((8, C), F32)
    for half in range(2):
        rows = w_up[:, half * C : (half + 1) * C].astype(F32)
        pre[0, half, 0] = jnp.concatenate([rows, zero8], axis=0).astype(BF)
        rows = w_head[:, half * EH : min((half + 1) * EH, E)].astype(F32)
        rows = jnp.concatenate([rows, jnp.zeros((24, C - rows.shape[1]), F32)], axis=1)
        pre[0, half, 1] = jnp.concatenate([rows, zero8], axis=0).astype(BF)
    text_buf[me_loop] = text[...].astype(F32)

    pl.semaphore_wait(barrier, N_DP - 1 + 2 * (N_LOOP - 1) + 1)

    def whole(ref, sem, recv_sem=None):
        return remote(ref, ref, sem, sem if recv_sem is None else recv_sem, me_loop, sib_dp)

    parity = lax.rem(me_loop // 2, 2)
    mix_of = (0, parity, 1 - parity)

    def slab_of(w, owner_core, where):
        if w == 0:
            return up_buf.at[owner_core, where]
        return mix_buf.at[mix_of[w], where, owner_core]

    def to_sibling(w, where):
        slab = slab_of(w, core, where)
        remote(slab, slab, bulk_send.at[w], bulk_recv.at[w], me_loop, sib_dp).start()

    def to_x(w, where_z, sem):
        slab = slab_of(w, core, where_z * 2 + xlo)
        side = lax.rem(where_z, 2)
        target = me_loop + side * (loop_b - me_loop)
        remote(slab, slab, x_send.at[w], w_recv.at[w, sem], target, xnb_dp).start()

    def to_z(w, where_z, direction, sem):
        slab = slab_of(w, core, where_z * 2 + xlo)
        remote(
            slab, slab, z_send.at[w], w_recv.at[w, sem], me_loop, z_dp(direction * sgn)
        ).start()

    def to_y(where, sem):
        slab = slab_of(1, core, where)
        target = lax.rem(me_loop + 2 * sgn + N_LOOP, N_LOOP)
        remote(slab, slab, y_send, y_recv.at[sem], target, me_dp).start()

    def await_slab(w, where, sem):
        slab = slab_of(w, core, where)
        remote(slab, slab, w_send, w_recv.at[w, sem], me_loop, sib_dp).wait_recv()

    def kind_z(kind):
        offset = -kind if kind <= 4 else kind - 4
        return lax.rem(zed + offset * sgn + N_Z, N_Z)

    def begin(w):
        to_z(w, zed, 1, 0)
        to_z(w, zed, -1, 4)
        to_x(w, zed, 7)
        if w == 1:
            to_y(chip, 0)
        to_sibling(w, chip)

    def z_arrival(w, kind):
        sem = kind - 1
        where_z = kind_z(kind)
        await_slab(w, where_z * 2 + xlo, sem)
        if kind in (1, 2, 3):
            to_z(w, where_z, 1, sem + 1)
        if kind in (5, 6):
            to_z(w, where_z, -1, sem + 1)
        to_x(w, where_z, 7 + kind)
        if w == 1:
            to_y(where_z * 2 + xlo, kind)
        to_sibling(w, where_z * 2 + xlo)

    def x_arrival(w, kind):
        where = kind_z(kind) * 2 + 1 - xlo
        await_slab(w, where, 7 + kind)
        if w == 1:
            to_y(where, 8 + kind)
        to_sibling(w, where)

    def y_arrival(index):
        side = xlo if index < 8 else 1 - xlo
        where = kind_z(index % 8) * 2 + side
        slab = slab_of(2, core, where)
        remote(slab, slab, y_send, y_recv.at[index], me_loop, sib_dp).wait_recv()
        to_sibling(2, where)

    def kinds_at(step):
        z_kinds = [step] if step <= 4 else []
        z_kinds += [4 + step] if step <= 3 else []
        x_kinds = {1: [0], 5: [4]}.get(step, [step - 1, 3 + step])
        return z_kinds, x_kinds

    def turn(w, step):
        if w == 2 and step == 0:
            y_arrival(0)
            return
        z_kinds, x_kinds = kinds_at(step)
        for kind in z_kinds:
            if w == 2:
                y_arrival(kind)
            else:
                z_arrival(w, kind)
        for kind in x_kinds:
            if w == 2:
                y_arrival(8 + kind)
            else:
                x_arrival(w, kind)

    def sixteen(w):
        return up_buf.at[0] if w == 0 else mix_buf.at[0, :, 0]

    def finish(w):
        whole(sixteen(w), bulk_send.at[w], bulk_recv.at[w]).wait_recv()

    pre_copy = remote(
        pre.at[0, 1 - core], pre.at[1, 0], pre_sem.at[0], pre_sem.at[1], me_loop, sib_dp
    )
    pre_copy.start()

    def text_copy(o):
        return remote(
            text_buf.at[me_loop],
            text_buf.at[me_loop],
            text_sem.at[0],
            text_sem.at[1],
            lax.rem(me_loop + o, N_LOOP),
            me_dp,
        )

    def merge(index):
        mine = pre[0, core, index].astype(F32)[:24]
        theirs = pre[1, 0, index].astype(F32)[:24]
        first = core == 0
        joined = jnp.concatenate(
            [jnp.where(first, mine, theirs), jnp.where(first, theirs, mine)], axis=0
        )
        return joined.astype(BF)

    pre_copy.wait_recv()
    up_buf[core, chip] = merge(0)
    begin(0)
    own_mix = jnp.where(parity == 0, w_down[...].astype(F32), merge(1).astype(F32))
    mix_buf[parity, chip, core] = own_mix.astype(BF)

    begin(1)

    width_at = lax.broadcasted_iota(jnp.int32, (16, 128), 0)

    def chunk_lanes(cb):
        return pl.ds(pl.multiple_of(cb * 128, 128), 128)

    def conv_chunk(chunk, carry):
        image, cb = chunk // 6, lax.rem(chunk, 6)
        lanes = chunk_lanes(cb)
        for a in range(7):
            for b in range(7):
                taps[a * 7 + b] = jnp.broadcast_to(kern[a, pl.ds(b, 1), lanes], (8, 128))

        def row(r, state):
            accs, total = state
            x = images[image, r, :, lanes].astype(F32)
            views = []
            for b in range(7):
                if b == 3:
                    view = x
                else:
                    view = pltpu.roll(x, (3 - b) % 16, 0)
                    inside = width_at >= 3 - b if b < 3 else width_at < 19 - b
                    view = jnp.where(inside, view, 0.0)
                shifted[chunk, b, r] = view
                views.append(view.reshape(2, 8, 128))
            fresh = []
            for j in range(7):
                acc = accs[j]
                for b in range(7):
                    acc = acc + views[b] * taps[(6 - j) * 7 + b]
                fresh.append(acc)
            conv_pad[image, r, :, lanes] = fresh[0].reshape(16, 128)
            return (tuple(fresh[1:]) + (jnp.zeros((2, 8, 128), F32),), total + views[3])

        zero = jnp.zeros((2, 8, 128), F32)
        accs, total = lax.fori_loop(0, 16, row, ((zero,) * 7, zero))
        for j in range(3):
            conv_pad[image, 16 + j, :, lanes] = accs[j].reshape(16, 128)
        img_sum[image, :, lanes] = total[0] + total[1]
        return carry

    plan = (
        ((0, 1), (1, 1)),
        ((0, 2), (1, 2), (2, 0)),
        ((0, 3), (1, 3), (2, 1)),
        ((0, 4), (1, 4), (2, 2)),
        ((0, 5), (1, 5), (2, 3)),
        ((2, 4),),
    )
    for group in range(6):
        lax.fori_loop(2 * group, 2 * group + 2, conv_chunk, 0)
        for w, step in plan[group]:
            turn(w, step)

    @pl.loop(1, N_LOOP)
    def _(o):
        text_copy(o).start()

    gain_row = gain[...].reshape(1, C)

    def norm_rows(index, carry):
        image, r = index // 16, lax.rem(index, 16)
        rows = pl.ds(pl.multiple_of(index * 16, 16), 16)
        value = conv_pad[image, r + 3]
        centered = value - jnp.mean(value, axis=-1, keepdims=True)
        inv = lax.rsqrt(jnp.mean(centered * centered, axis=-1, keepdims=True) + EPS)
        hat = centered * inv
        xhat[rows, :] = hat
        rstd[rows, :] = jnp.broadcast_to(inv, (16, 128))
        normed[rows, :] = (hat * gain_row).astype(BF)
        return carry

    lax.fori_loop(0, 32, norm_rows, 0)
    finish(0)

    scale_row = scale[...].reshape(1, C)
    c0 = 0.7978845608028654
    row_at = lax.broadcasted_iota(jnp.int32, (16, C), 0)
    means = []
    for half in range(2):
        hid[...] = jnp.dot(
            normed[...], up_buf[half].reshape(C, C), preferred_element_type=F32
        )
        if half == 0:
            turn(2, 5)
        bias = b_up[half * C : (half + 1) * C].reshape(1, C)
        image_sums = []
        for image in range(2):

            def gelu_rows(index, total):
                rows = pl.ds(pl.multiple_of(image * 256 + index * 16, 16), 16)
                h = hid[rows, :] + bias
                square = h * h
                t = jnp.tanh(c0 * h * (1.0 + 0.044715 * square))
                plus = 0.5 + 0.5 * t
                active = (h * plus).astype(BF).astype(F32)
                gprime[half, rows, :] = plus + (0.5 * c0) * h * (1.0 - t * t) * (
                    1.0 + (3 * 0.044715) * square
                )
                return total + active[:8] + active[8:]

            total = lax.fori_loop(0, 16, gelu_rows, jnp.zeros((8, C), F32))
            image_sums.append(jnp.sum(total, axis=0, keepdims=True) * (1.0 / 256))
        means.append(
            jnp.where(row_at == 0, image_sums[0], jnp.where(row_at == 1, image_sums[1], 0.0))
        )

    whole(text_buf.at[pl.ds(0, N_LOOP - 1)], text_sem.at[0], text_sem.at[1]).wait_recv()
    for l in range(N_LOOP):
        text_all[2 * l : 2 * l + 2, :] = text_buf[l]
    raw_rows = text_all[...]
    text_norm = jnp.sqrt(jnp.sum(raw_rows * raw_rows, axis=-1, keepdims=True) + EPS)
    text_emb = (raw_rows / text_norm).astype(BF).astype(F32)
    logit_scale = jnp.exp(jnp.full((1, 1), log_temp[0], F32))
    img_mean = [jnp.sum(img_sum[image], axis=0, keepdims=True) * (1.0 / 256) for image in range(2)]
    img_mean = jnp.where(row_at == 0, img_mean[0], jnp.where(row_at == 1, img_mean[1], 0.0))
    finish(1)
    finish(2)
    mlp = jnp.zeros((16, C), F32)
    for half in range(2):
        high = means[half].astype(BF)
        low = (means[half] - high.astype(F32)).astype(BF)
        rows = mix_buf[0, 8 * half : 8 * half + 8].reshape(C, C)
        mlp = mlp + jnp.dot(high, rows, preferred_element_type=F32)
        mlp = mlp + jnp.dot(low, rows, preferred_element_type=F32)
    pooled = (img_mean + scale_row * mlp).astype(BF)
    raw = [
        jnp.dot(
            pooled, mix_buf[1, :, half, :, :EH].reshape(C, EH), preferred_element_type=F32
        )
        for half in range(2)
    ]
    norm = lax.rsqrt(
        jnp.sum(raw[0] * raw[0], axis=-1, keepdims=True)
        + jnp.sum(raw[1] * raw[1], axis=-1, keepdims=True)
        + EPS
    )
    emb = jnp.concatenate([raw[0] * norm, raw[1][:, : E - EH] * norm], axis=1)

    logits = logit_scale * nt(emb, text_emb, HI) + loss_bias[0]
    pair_row_at = lax.broadcasted_iota(jnp.int32, (16, GROUP), 0)
    pair_col_at = lax.broadcasted_iota(jnp.int32, (16, GROUP), 1)
    own = jnp.where(pair_row_at == 0, pair[0, 0], pair[0, 1])
    signs = jnp.where(own == pair_col_at, 1.0, -1.0)
    weight = -signs * jax.nn.sigmoid(-signs * logits) / GROUP
    weight = jnp.where(pair_row_at < 2, weight, 0.0)
    image_cot = logit_scale * jnp.dot(weight, text_emb, precision=HI, preferred_element_type=F32)

    msg_buf[me_loop, :, :E] = emb[:2]
    msg_buf[me_loop, :, E:] = jnp.concatenate(
        [weight[:2], jnp.zeros((2, 128 - GROUP), F32)], axis=1
    )

    def msg_copy(o):
        return remote(
            msg_buf.at[me_loop],
            msg_buf.at[me_loop],
            msg_sem.at[0],
            msg_sem.at[1],
            lax.rem(me_loop + o, N_LOOP),
            me_dp,
        )

    d_raw = norm * (image_cot - emb * jnp.sum(image_cot * emb, axis=-1, keepdims=True))
    d_raw = d_raw.astype(BF)
    d_pooled = nt(d_raw[:, :EH], mix_buf[1, :, 0, :, :EH].reshape(C, EH)) + nt(
        d_raw[:, EH:], mix_buf[1, :, 1, :, : E - EH].reshape(C, E - EH)
    )
    d_pooled = d_pooled.astype(BF).astype(F32)
    d_mlp = (scale_row * (d_pooled * (1.0 / 256))).astype(BF)
    for half in range(2):
        value = nt(d_mlp, mix_buf[0, 8 * half : 8 * half + 8].reshape(C, C))
        dact[half] = value.astype(BF).astype(F32)

    def hidden_cot(half):
        for image in range(2):
            factor = dact[half, image : image + 1, :]

            def rows_cot(index, carry):
                rows = pl.ds(pl.multiple_of(image * 256 + index * 16, 16), 16)
                dhid[half, rows, :] = (gprime[half, rows, :] * factor).astype(BF)
                return carry

            lax.fori_loop(0, 16, rows_cot, 0)

    def up_grad_half(half):
        hidden_cot(half)
        g_buf[half] = tn(normed[...], dhid[half]).astype(BF).reshape(16, 48, C)

    up_grad_half(1 - core)
    r1 = remote(g_buf.at[1 - core], rs1, r1_sem.at[0], r1_sem.at[1], me_loop, sib_dp)
    r1.start()
    up_grad_half(core)
    r1.wait_recv()

    def core_sum(where):
        s1[where] = (g_buf[core, where].astype(F32) + rs1[where].astype(F32)).astype(BF)

    def x_copy(z):
        where = z * 2 + 1 - xlo
        target = me_loop + lax.rem(z, 2) * (loop_b - me_loop)
        return remote(s1.at[where], rs2.at[z], r2_send, r2_recv.at[z], target, xnb_dp)

    @pl.loop(1, N_Z + 1)
    def _(o):
        z = lax.rem(zed + o, N_Z)
        core_sum(z * 2 + 1 - xlo)
        x_copy(z).start()

    @pl.loop(0, N_Z)
    def _(z):
        core_sum(z * 2 + xlo)

    @pl.loop(1, N_LOOP)
    def _(o):
        msg_copy(o).start()

    hid[...] = nt(dhid[0], up_buf[0].reshape(C, C)) + nt(dhid[1], up_buf[1].reshape(C, C))

    dconv = conv_pad

    def norm_cot(index, carry):
        rows = pl.ds(pl.multiple_of(index * 16, 16), 16)
        d_hat = hid[rows, :].astype(BF).astype(F32) * gain_row
        hat = xhat[rows, :]
        first = jnp.mean(d_hat, axis=-1, keepdims=True)
        second = jnp.mean(d_hat * hat, axis=-1, keepdims=True)
        dconv[index // 16, lax.rem(index, 16)] = rstd[rows, :1] * (
            d_hat - first - hat * second
        )
        return carry

    lax.fori_loop(0, 32, norm_cot, 0)

    def z_copy(o):
        z = lax.rem(zed + o, N_Z)
        return remote(
            s2.at[z],
            rs3.at[o - 1],
            r3_sem.at[0],
            r3_sem.at[1],
            me_loop,
            z * 4 + xlo * 2 + core,
        )

    def x_sum(z):
        x_copy(z).wait_recv()
        s2[z] = (s1[z * 2 + xlo].astype(F32) + rs2[z].astype(F32)).astype(BF)

    @pl.loop(1, N_Z)
    def _(o):
        x_sum(lax.rem(zed + o, N_Z))
        z_copy(o).start()

    x_sum(zed)

    kg[...] = jnp.zeros(kg.shape, F32)

    summing = (chip < N_SLAB) & (core == lax.rem(chip, 2))

    def slab_copy(slab):
        return remote(
            kg_out.at[slab],
            kr1.at[me_dp],
            p1_sem.at[0],
            p1_sem.at[1],
            me_loop,
            2 * slab + slab % 2,
        )

    tap_at = lax.broadcasted_iota(jnp.int32, (8, 128), 0)

    def kernel_chunk(cb, offset):
        lanes = chunk_lanes(cb)

        def column(b, carry):
            accs = [jnp.zeros((2, 8, 128), F32) for _ in range(7)]
            for image in range(2):
                window = {}
                for r in range(16):
                    view = shifted[image * 6 + cb, b, r].reshape(2, 8, 128)
                    for a in range(7):
                        h = r - a + 3
                        if 0 <= h < 16:
                            if h not in window:
                                value = dconv[image, h, :, lanes]
                                window[h] = value.reshape(2, 8, 128)
                            accs[a] = accs[a] + view * window[h]
            pair = cb // 2
            for a in range(7):
                value = jnp.sum(accs[a][0] + accs[a][1], axis=0, keepdims=True)
                columns = slice(offset, offset + 128)
                kg[pair, a, :, columns] = kg[pair, a, :, columns] + jnp.where(
                    tap_at == b, value, 0.0
                )
            return carry

        lax.fori_loop(0, 7, column, 0)

    for group in range(3):
        kernel_chunk(2 * group, 0)
        kernel_chunk(2 * group + 1, 128)
        for part in range(4):
            slab = group * 4 + part
            kg_out[slab] = kg[group, 2 * part : 2 * part + 2].reshape(16, 256).astype(BF)

            @pl.when(jnp.logical_not(summing) | (chip != slab))
            def _():
                slab_copy(slab).start()

    def share_copy(o):
        return remote(
            kr2.at[me_loop],
            kr2.at[me_loop],
            p2_sem.at[0],
            p2_sem.at[1],
            lax.rem(me_loop + o, N_LOOP),
            me_dp,
        )

    def spread_copy(o):
        return remote(
            k1, kfin.at[chip], p3_sem.at[0], p3_sem.at[1], me_loop, lax.rem(me_dp + o, N_DP)
        )

    def sum_dp(first, last):
        @pl.when(summing & (chip >= first) & (chip < last))
        def _():
            whole(kr1.at[pl.ds(0, N_DP - 1)], p1_sem.at[0], p1_sem.at[1]).wait_recv()
            kr1[me_dp] = kg_out[chip]
            summed = kr1[0].astype(F32)
            for d in range(1, N_DP):
                summed = summed + kr1[d].astype(F32)
            kr2[me_loop] = summed.astype(BF)

            @pl.loop(1, N_LOOP)
            def _(o):
                share_copy(o).start()

    def sum_loop(first, last):
        @pl.when(summing & (chip >= first) & (chip < last))
        def _():
            whole(kr2.at[pl.ds(0, N_LOOP - 1)], p2_sem.at[0], p2_sem.at[1]).wait_recv()
            summed = kr2[0].astype(F32)
            for l in range(1, N_LOOP):
                summed = summed + kr2[l].astype(F32)
            k1[...] = summed.astype(BF)

            @pl.loop(1, N_DP)
            def _(o):
                spread_copy(o).start()

            kfin[chip] = summed.astype(BF)

    sum_dp(0, 8)

    pre_copy.wait_send()
    for w in range(3):
        whole(sixteen(w), bulk_send.at[w]).wait_send()
    for w in range(2):
        whole(up_buf.at[0, pl.ds(0, 7)], z_send.at[w]).wait_send()
        whole(up_buf.at[0, pl.ds(0, 8)], x_send.at[w]).wait_send()
    whole(sixteen(0), y_send).wait_send()
    whole(text_buf.at[pl.ds(0, N_LOOP - 1)], text_sem.at[0]).wait_send()

    whole(msg_buf.at[pl.ds(0, N_LOOP - 1)], msg_sem.at[0], msg_sem.at[1]).wait_recv()
    for l in range(N_LOOP):
        msg_all[2 * l : 2 * l + 2, :] = msg_buf[l]
    all_emb = msg_all[:, :E]
    all_weight = msg_all[:, E:]
    pick_row = lax.broadcasted_iota(jnp.int32, (8, 128), 0)
    pick_col = lax.broadcasted_iota(jnp.int32, (8, 128), 1)
    pick = jnp.where((pick_col == 2 * me_loop + pick_row) & (pick_row < 2), 1.0, 0.0)
    mine = nt(pick, all_weight, HI)
    text_cot = logit_scale * jnp.dot(mine, all_emb, precision=HI, preferred_element_type=F32)
    text_cot = text_cot[:2]
    own_rows = text[...].astype(F32)
    own_norm = jnp.sqrt(jnp.sum(own_rows * own_rows, axis=-1, keepdims=True) + EPS)
    own_hat = own_rows / own_norm
    text_out[...] = (
        text_cot - own_hat * jnp.sum(own_hat * text_cot, axis=-1, keepdims=True)
    ) / own_norm

    total = s2[zed].astype(F32)
    whole(rs3, r3_sem.at[0], r3_sem.at[1]).wait_recv()
    for o in range(1, N_Z):
        total = total + rs3[o - 1].astype(F32)
    for q in range(N_PIECE):
        rb, lh = q // 2, q % 2
        p3[q] = total[rb * 8 : rb * 8 + 8, lh * 384 : lh * 384 + 384]

    def piece_copy(q):
        return remote(p3.at[q], rs4.at[me_loop], r4_sem.at[0], r4_sem.at[1], q, me_dp)

    for q in range(N_PIECE):

        @pl.when(me_loop != q)
        def _():
            piece_copy(q).start()

    sum_dp(8, N_SLAB)
    sum_loop(0, 8)

    target_core = me_loop // 6
    target_dp = chip * 2 + target_core
    own_piece = lax.rem(me_loop, 6)

    def result_copy(o):
        return remote(
            r4,
            fin.at[core * 6 + own_piece],
            r5_sem.at[0],
            r5_sem.at[1],
            lax.rem(me_loop + o, N_LOOP),
            target_dp,
        )

    @pl.when(me_loop < N_PIECE)
    def _():
        whole(rs4.at[pl.ds(0, N_LOOP - 1)], r4_sem.at[0], r4_sem.at[1]).wait_recv()
        rs4[me_loop] = p3[me_loop]
        summed = rs4[0]
        for l in range(1, N_LOOP):
            summed = summed + rs4[l]
        r4[...] = summed

        @pl.loop(1, N_LOOP)
        def _(o):
            result_copy(o).start()

        @pl.when(target_core != core)
        def _():
            remote(
                r4,
                fin.at[core * 6 + own_piece],
                r5_sem.at[0],
                r5_sem.at[1],
                me_loop,
                sib_dp,
            ).start()

        @pl.when(target_core == core)
        def _():
            fin[core * 6 + own_piece] = r4[...]

    sum_loop(8, N_SLAB)

    own_result = (target_core == core) & (me_loop < N_PIECE)

    @pl.when(own_result)
    def _():
        whole(fin.at[pl.ds(0, N_PIECE - 1)], r5_sem.at[0], r5_sem.at[1]).wait_recv()

    @pl.when(jnp.logical_not(own_result))
    def _():
        whole(fin, r5_sem.at[0], r5_sem.at[1]).wait_recv()

    for cs in range(2):
        for j in range(6):
            rb, lh = j // 2, j % 2
            columns = slice(cs * C + lh * 384, cs * C + lh * 384 + 384)
            up_out[rb * 8 : rb * 8 + 8, columns] = fin[cs * 6 + j]

    @pl.when(summing)
    def _():
        some = pl.ds(0, N_SLAB - 1)
        whole(kfin.at[some], p3_sem.at[0], p3_sem.at[1]).wait_recv()
        whole(kg_out.at[some], p1_sem.at[0]).wait_send()
        whole(kr2.at[pl.ds(0, N_LOOP - 1)], p2_sem.at[0]).wait_send()
        whole(kr1.at[pl.ds(0, N_DP - 1)], p3_sem.at[0]).wait_send()

    @pl.when(jnp.logical_not(summing))
    def _():
        whole(kfin, p3_sem.at[0], p3_sem.at[1]).wait_recv()
        whole(kg_out, p1_sem.at[0]).wait_send()

    for slab in range(N_SLAB):
        lp, part = slab // 4, slab % 4
        value = kfin[slab].astype(F32)
        kernel_out[2 * part, :, lp * 256 : lp * 256 + 256] = value[:7]
        if part < 3:
            kernel_out[2 * part + 1, :, lp * 256 : lp * 256 + 256] = value[8:15]

    whole(msg_buf.at[pl.ds(0, N_LOOP - 1)], msg_sem.at[0]).wait_send()
    r1.wait_send()
    whole(rs2, r2_send).wait_send()
    whole(rs3, r3_sem.at[0]).wait_send()

    @pl.when(me_loop < N_PIECE)
    def _():
        whole(p3.at[pl.ds(0, N_PIECE - 1)], r4_sem.at[0]).wait_send()

        @pl.when(target_core != core)
        def _():
            whole(rs4, r5_sem.at[0]).wait_send()

        @pl.when(target_core == core)
        def _():
            whole(rs4.at[pl.ds(0, N_LOOP - 1)], r5_sem.at[0]).wait_send()

    @pl.when(me_loop >= N_PIECE)
    def _():
        whole(p3, r4_sem.at[0]).wait_send()


def body(
    images,
    kernel,
    ln_gain,
    w_up,
    b_up,
    w_down,
    layer_scale,
    w_head,
    text_rows,
    pair_ids,
    log_temp,
    loss_bias,
):
    vmem = pl.BlockSpec(memory_space=pltpu.VMEM)
    smem = pl.BlockSpec(memory_space=pltpu.SMEM)
    dma = pltpu.SemaphoreType.DMA
    scratch = [
        pltpu.VMEM((2, 2, 2, 32, C), BF),
        pltpu.VMEM((2, 16, 48, C), BF),
        pltpu.VMEM((2, 16, 2, 48, C), BF),
        pltpu.VMEM((N_LOOP, 2, E), F32),
        pltpu.VMEM((GROUP, E), F32),
        pltpu.VMEM((49, 8, 128), F32),
        pltpu.VMEM((12, 7, 16, 16, 128), F32),
        pltpu.VMEM((2, 19, 16, C), F32),
        pltpu.VMEM((2, 8, C), F32),
        pltpu.VMEM((512, C), BF),
        pltpu.VMEM((512, C), F32),
        pltpu.VMEM((512, 128), F32),
        pltpu.VMEM((512, C), F32),
        pltpu.VMEM((2, 512, C), F32),
        pltpu.VMEM((2, 16, C), F32),
        pltpu.VMEM((2, 512, C), BF),
        pltpu.VMEM((2, 16, 48, C), BF),
        pltpu.VMEM((16, 48, C), BF),
        pltpu.VMEM((16, 48, C), BF),
        pltpu.VMEM((8, 48, C), BF),
        pltpu.VMEM((8, 48, C), BF),
        pltpu.VMEM((7, 48, C), BF),
        pltpu.VMEM((N_PIECE, 8, 384), F32),
        pltpu.VMEM((N_LOOP, 8, 384), F32),
        pltpu.VMEM((8, 384), F32),
        pltpu.VMEM((N_PIECE, 8, 384), F32),
        pltpu.VMEM((N_LOOP, 2, E + 128), F32),
        pltpu.VMEM((GROUP, E + 128), F32),
        pltpu.VMEM((3, 8, 8, 256), F32),
        pltpu.VMEM((N_SLAB, 16, 256), BF),
        pltpu.VMEM((N_DP, 16, 256), BF),
        pltpu.VMEM((16, 256), BF),
        pltpu.VMEM((N_LOOP, 16, 256), BF),
        pltpu.VMEM((N_SLAB, 16, 256), BF),
        dma,
        dma((2, 15)),
        dma((3,)),
        dma((3,)),
        dma((2,)),
        dma((2,)),
        dma,
        dma((16,)),
        dma((2,)),
        dma((2,)),
        dma((2,)),
        dma((2,)),
        dma,
        dma((N_Z,)),
        dma((2,)),
        dma((2,)),
        dma((2,)),
        dma((2,)),
        dma((2,)),
        dma((2,)),
    ]
    kernel_grad, up_grad, text_grad = pl.pallas_call(
        kernel_body,
        out_shape=(
            jax.ShapeDtypeStruct((7, 7, C), F32),
            jax.ShapeDtypeStruct((24, FFW), F32),
            jax.ShapeDtypeStruct((2, E), F32),
        ),
        in_specs=[vmem] * 9 + [smem] * 3,
        out_specs=(vmem, vmem, vmem),
        scratch_shapes=scratch,
        compiler_params=pltpu.CompilerParams(
            collective_id=0, has_side_effects=True, vmem_limit_bytes=56 * 1024 * 1024
        ),
        name="tower_step",
    )(
        images[0],
        kernel,
        ln_gain,
        w_up,
        b_up,
        w_down,
        layer_scale,
        w_head,
        text_rows[0],
        pair_ids,
        log_temp,
        loss_bias,
    )
    return (kernel_grad, up_grad, text_grad[None])


def solution(mesh):
    placed = (
        P("dp", "loop", None, None, None),
        P(),
        P(),
        P("dp", None),
        P(),
        P("dp", None),
        P(),
        P("dp", None),
        P("dp", "loop", None),
        P("dp", "loop"),
        P(),
        P(),
    )
    return jax.shard_map(
        body,
        mesh=mesh,
        in_specs=placed,
        out_specs=(P(), P("dp", None), P("dp", "loop", None)),
        check_vma=False,
    )
```
